32 devices in a mesh: ball: 4 (over y, x), region: 8 (over z, core).
Axes of the slice: x: 2, y: 2, z: 4, core: 2. Of those that a mesh axis runs over, the one named last changes fastest.
Arguments:
- points: bfloat16 [4, 8, 1024, 256], P('ball', 'region'), may hold values from -6 to 6
- gain_attn: float32 [256], replicated, may hold values from 0.1 to 1.9
- w_query_key: bfloat16 [256, 512], replicated, may hold values from -7 to 7
- w_value: bfloat16 [256, 256], replicated, may hold values from -0.375 to 0.375
- w_out: bfloat16 [256, 256], replicated, may hold values from -0.375 to 0.375
- gain_mlp: float32 [256], replicated, may hold values from 0.1 to 1.9
- w_up: bfloat16 [256, 1024], replicated, may hold values from -0.375 to 0.375
- w_down: bfloat16 [1024, 256], replicated, may hold values from -0.1875 to 0.1875
- cluster_dest: int32 [4, 8, 16], P('ball', 'region'), may hold values from 0 to 63, as said below
Outputs:
- block_out: bfloat16 [4, 8, 1024, 256], P('ball', 'region')
The draws below stay inside these ranges and needn't reach their ends.
Inputs may be any that keep to these rules, and one draw needn't show every extreme that they name: cluster_dest[l, r, c] = o * 16 + s sends cluster c of lane l, region r to slot s of lane o, region r. Within one region all values are distinct. Each lane sends exactly 8 clusters to each of 2 owner lanes and none to the others, and the offsets (o - l) mod 4 of those owners are the same set for every lane of one region.
All inputs are finite; a program needn't handle non-finite values.
Results may differ from the reference program's by a relative error of at most 0.012.
The reference program's roundings to bfloat16 on the way count: a program that leaves them out, or rounds other values in their place, can miss the bound.
Values may be sent and summed in bfloat16 or wider, within the bound.
No kernel may reach another device: no remote copies, remote signals or barrier semaphores. Data moves between devices by JAX's collectives and lax.ppermute only.
A program may use at most 64 MiB of HBM per device.

```python
import math
import jax
import jax.numpy as jnp
from jax import lax

C = 256
HEADS = 8
MLP_HID = 1024
BALL = 1024
CLUSTER = 64
POOL = 16
PTS_DEV = 1024
CLUS_DEV = 16
LANES = 4
REGIONS = 8
CAP = 8


def draw_points(key, part):
    shape = (LANES, REGIONS, PTS_DEV, C)
    key_base = jax.random.fold_in(key, 0)
    base = jax.random.normal(key_base, shape, jnp.float32)
    return jnp.clip(base, -6.0, 6.0).astype(jnp.bfloat16)


def draw_w_query_key(key, part):
    key_query, key_keys = jax.random.split(key, 2)
    factor = 2.0 / math.sqrt(C)
    query_part = jnp.clip(jax.random.normal(key_query, (C, C), jnp.float32), -4.0, 4.0) * factor
    key_part = jnp.clip(jax.random.normal(key_keys, (C, C), jnp.float32), -4.0, 4.0) * factor
    return jnp.clip(jnp.concatenate([query_part, key_part], axis=1), -7.0, 7.0).astype(jnp.bfloat16)


def draw_cluster_dest(key, part):
    half = LANES // 2
    key_offsets, key_order, key_slots = jax.random.split(key, 3)
    offset_scores = jax.random.randint(key_offsets, (REGIONS, LANES), 0, 1 << 20) * LANES + jnp.arange(LANES, dtype=jnp.int32)[None, :]
    chosen = jnp.sort(jnp.argsort(offset_scores, axis=1)[:, :half], axis=1).astype(jnp.int32)
    region_ids = jnp.arange(REGIONS, dtype=jnp.int32)[:, None]
    member = jnp.zeros((REGIONS, LANES), jnp.int32).at[region_ids, chosen].set(1)
    sources = jnp.arange(LANES, dtype=jnp.int32)
    offsets_table = (sources[None, :] - sources[:, None]) % LANES
    sends = member[:, offsets_table]
    source_rank = jnp.cumsum(sends, axis=1) - sends
    order_scores = jax.random.randint(key_order, (REGIONS, LANES, CLUS_DEV), 0, 1 << 20) * CLUS_DEV + jnp.arange(CLUS_DEV, dtype=jnp.int32)
    position = jnp.argsort(jnp.argsort(order_scores, axis=2), axis=2).astype(jnp.int32)
    chosen_wide = jnp.broadcast_to(chosen[:, None, :], (REGIONS, LANES, half))
    offset = jnp.take_along_axis(chosen_wide, position // CAP, axis=2)
    owner = (sources[None, :, None] + offset) % LANES
    within = position % CAP
    arrival = jnp.take_along_axis(source_rank, owner, axis=2) * CAP + within
    slot_scores = jax.random.randint(key_slots, (REGIONS, LANES, CLUS_DEV), 0, 1 << 20) * CLUS_DEV + jnp.arange(CLUS_DEV, dtype=jnp.int32)
    slot_perm = jnp.argsort(slot_scores, axis=2).astype(jnp.int32).reshape(REGIONS, LANES * CLUS_DEV)
    slot_index = (owner * CLUS_DEV + arrival).reshape(REGIONS, LANES * CLUS_DEV)
    slots = jnp.take_along_axis(slot_perm, slot_index, axis=1).reshape(REGIONS, LANES, CLUS_DEV)
    destination = owner * CLUS_DEV + slots
    return destination.transpose(1, 0, 2).astype(jnp.int32)


def gaussian(key, dims, spread, limit, held_as=jnp.bfloat16):
    entries = jax.random.normal(key, dims, jnp.float32) * spread
    return jnp.minimum(jnp.maximum(entries, -limit), limit).astype(held_as)


def setup_inputs(seed: int = 0) -> dict:
    key_list = jax.random.split(jax.random.key(seed), 10)
    return {
        "points": draw_points(jax.random.fold_in(key_list[9], 71), 0),
        "gain_attn": jnp.clip(1.0 + 0.18 * jax.random.normal(key_list[1], (C,), jnp.float32), 0.1, 1.9),
        "w_query_key": draw_w_query_key(jax.random.fold_in(key_list[9], 71), 0),
        "w_value": gaussian(key_list[3], (C, C), C ** -0.5, 0.375),
        "w_out": gaussian(key_list[4], (C, C), C ** -0.5, 0.375),
        "gain_mlp": jnp.clip(1.0 + 0.18 * jax.random.normal(key_list[5], (C,), jnp.float32), 0.1, 1.9),
        "w_up": gaussian(key_list[6], (C, MLP_HID), C ** -0.5, 0.375),
        "w_down": gaussian(key_list[7], (MLP_HID, C), MLP_HID ** -0.5, 0.1875),
        "cluster_dest": draw_cluster_dest(jax.random.fold_in(key_list[9], 71), 0),
    }


def rms_norm(row_data, gain_vector):
    widened = row_data.astype(jnp.float32)
    scaling = lax.rsqrt(lax.optimization_barrier(jnp.mean(widened * widened, axis=1, keepdims=True)) + 1e-06)
    return (widened * scaling * gain_vector.astype(jnp.float32)).astype(jnp.bfloat16)

def attend(query, keys, values):
    row_count, columns = query.shape
    head_size = columns // HEADS
    row_block = min(512, row_count)
    query_heads = query.reshape(row_count // row_block, row_block, HEADS, head_size).transpose(2, 0, 1, 3)
    key_heads = keys.reshape(-1, HEADS, head_size).transpose(1, 0, 2)
    value_heads = values.reshape(-1, HEADS, head_size).transpose(1, 0, 2)

    def one_head(operands):
        query_blocks, key_head, value_head = operands

        def one_block(query_block):
            scores = jnp.einsum('nd,md->nm', query_block.astype(jnp.float32), key_head.astype(jnp.float32)) / math.sqrt(head_size)
            row_max = lax.optimization_barrier(jnp.max(scores, axis=1, keepdims=True))
            exponent = jnp.exp(scores - row_max)
            weights = (exponent / lax.optimization_barrier(jnp.sum(exponent, axis=1, keepdims=True))).astype(jnp.bfloat16)
            mixed = jnp.einsum('nm,md->nd', weights.astype(jnp.float32), value_head.astype(jnp.float32))
            return mixed.astype(jnp.bfloat16)
        return lax.map(one_block, query_blocks)
    result = lax.map(one_head, (query_heads, key_heads, value_heads))
    return result.transpose(1, 2, 0, 3).reshape(row_count, columns)

def reference(points, gain_attn, w_query_key, w_value, w_out, gain_mlp, w_up, w_down, cluster_dest):
    lanes, regions, per_device, columns = points.shape
    clusters = per_device // CLUSTER
    flat = points.reshape(-1, columns)
    normed = rms_norm(flat, gain_attn)
    paired = jnp.dot(normed, w_query_key, preferred_element_type=jnp.float32).astype(jnp.bfloat16)
    query = paired[:, :columns]
    keys = paired[:, columns:]
    values = jnp.dot(normed, w_value, preferred_element_type=jnp.float32).astype(jnp.bfloat16)

    def pooled(source):
        summed = lax.optimization_barrier(jnp.sum(source.reshape(-1, POOL, columns).astype(jnp.float32), axis=1))
        return (summed / math.sqrt(POOL)).astype(jnp.bfloat16).reshape(lanes, -1, columns)
    pooled_keys = pooled(keys)
    pooled_values = pooled(values)
    ball_count = flat.shape[0] // BALL
    per_lane = ball_count // lanes
    ball_indices = jnp.arange(ball_count, dtype=jnp.int32)

    def near_ball(index):
        start = index * BALL
        lane = index // per_lane
        ball_query = lax.dynamic_slice_in_dim(query, start, BALL, 0)
        ball_keys = lax.dynamic_slice_in_dim(keys, start, BALL, 0)
        ball_values = lax.dynamic_slice_in_dim(values, start, BALL, 0)
        lane_keys = lax.dynamic_index_in_dim(pooled_keys, lane, 0, keepdims=False)
        lane_values = lax.dynamic_index_in_dim(pooled_values, lane, 0, keepdims=False)
        return attend(ball_query, jnp.concatenate([ball_keys, lane_keys], axis=0), jnp.concatenate([ball_values, lane_values], axis=0))
    near = lax.map(near_ball, ball_indices).reshape(-1, columns)

    def by_region(source):
        inner = source.shape[1]
        return source.reshape(lanes, regions, clusters, CLUSTER * inner).transpose(1, 0, 2, 3).reshape(regions, lanes * clusters, CLUSTER * inner)

    def from_region(source, inner):
        return source.reshape(regions, lanes, clusters, CLUSTER * inner).transpose(1, 0, 2, 3).reshape(-1, inner)
    target = cluster_dest.transpose(1, 0, 2).reshape(regions, lanes * clusters).astype(jnp.int32)
    stacked = by_region(jnp.concatenate([query, keys, values], axis=1))
    placed = jax.vmap(lambda where_to, source: jnp.zeros_like(source).at[where_to].set(source))(target, stacked)
    rotated = from_region(placed, 3 * columns)

    def far_ball(index):
        ball_rows = lax.dynamic_slice_in_dim(rotated, index * BALL, BALL, 0)
        return attend(ball_rows[:, :columns], ball_rows[:, columns:2 * columns], ball_rows[:, 2 * columns:])
    far_rotated = lax.map(far_ball, ball_indices).reshape(-1, columns)
    far = from_region(jax.vmap(lambda where_to, source: source[where_to])(target, by_region(far_rotated)), columns)
    after = (flat.astype(jnp.float32) + jnp.dot(near, w_out, preferred_element_type=jnp.float32) + jnp.dot(far, w_out, preferred_element_type=jnp.float32)).astype(jnp.bfloat16)
    normed_mlp = rms_norm(after, gain_mlp)
    hidden = jax.nn.gelu(jnp.dot(normed_mlp, w_up, preferred_element_type=jnp.float32), approximate=True).astype(jnp.bfloat16)
    block_out = (after.astype(jnp.float32) + jnp.dot(hidden, w_down, preferred_element_type=jnp.float32)).astype(jnp.bfloat16)
    return block_out.reshape(points.shape)
```

```python
import functools
import math

import jax
import jax.numpy as jnp
from jax import lax
from jax.experimental import pallas as pl
from jax.experimental.pallas import tpu as pltpu
from jax.sharding import PartitionSpec as P

HEADS = 8
BALL = 1024
CLUSTER = 64
POOL = 16
LANE_TILE = 128
BLOCK = 512
VMEM_LIMIT = 48 * 1024 * 1024

bf16 = jnp.bfloat16
f32 = jnp.float32


def in_vmem():
    return pl.BlockSpec(memory_space=pltpu.VMEM)


def in_smem():
    return pl.BlockSpec(memory_space=pltpu.SMEM)


def anywhere():
    return pl.BlockSpec(memory_space=pl.ANY)


def params():
    return pltpu.CompilerParams(vmem_limit_bytes=VMEM_LIMIT)


def cost(flops, moved, transcendentals=0):
    return pl.CostEstimate(
        flops=int(flops), bytes_accessed=int(moved), transcendentals=int(transcendentals)
    )


def rms_norm(rows, gain):
    widened = rows.astype(f32)
    scaling = lax.rsqrt(jnp.mean(widened * widened, axis=1, keepdims=True) + 1e-06)
    return (widened * scaling * gain).astype(bf16)


def dot32(left, right):
    return jnp.dot(left, right, preferred_element_type=f32)


def owner_offset(dest_ref, cluster, clusters, lanes, me):
    owner = dest_ref[cluster] // clusters
    return lax.rem(owner - me + lanes, lanes)


def set_keys(kt_ref, first, keys):
    kt_ref[:, first : first + keys.shape[0]] = keys.T


def set_values(ve_ref, first, values):
    count, columns = values.shape
    for group in range(columns // LANE_TILE):
        ve_ref[group, first : first + count, :LANE_TILE] = values[
            :, group * LANE_TILE : (group + 1) * LANE_TILE
        ]
        ve_ref[group, first : first + count, LANE_TILE:] = jnp.ones((count, LANE_TILE), bf16)


def run_heads(jobs, query_of, kt_ref, ve_ref, head_size, finish):
    per_tile = LANE_TILE // head_size
    columns = kt_ref.shape[0]
    head_of_lane = lax.broadcasted_iota(jnp.int32, (1, columns), 1) // head_size
    factor = math.log2(math.e) / math.sqrt(head_size)

    def scores(job):
        tag, head, first, end = job
        masked = jnp.where(head_of_lane == head, query_of(tag), bf16(0))
        return dot32(masked, kt_ref[:, first:end])

    current = scores(jobs[0])
    for index, job in enumerate(jobs):
        following = scores(jobs[index + 1]) if index + 1 < len(jobs) else None
        tag, head, first, end = job
        row_max = jnp.max(current, axis=1, keepdims=True)
        weights = jnp.exp2((current - row_max) * factor).astype(bf16)
        mixed = dot32(weights, ve_ref[head // per_tile, first:end, :])
        finish(tag, head, mixed[:, :LANE_TILE], mixed[:, LANE_TILE:], row_max)
        current = following


def place_head(kept, head, per_tile, head_size, new):
    lane = lax.broadcasted_iota(jnp.int32, (1, LANE_TILE), 1) // head_size
    if kept is None:
        return jnp.broadcast_to(new, (new.shape[0], LANE_TILE))
    return jnp.where(lane == head % per_tile, new, kept)


def full_attention(jobs, query_of, kt_ref, ve_ref, columns, out_of):
    head_size = columns // HEADS
    per_tile = LANE_TILE // head_size
    kept = {}

    def finish(tag, head, mixed, total, row_max):
        group = head // per_tile
        kept[tag, group] = place_head(
            kept.get((tag, group)), head, per_tile, head_size, mixed / total
        )
        if head % per_tile == per_tile - 1:
            out_of(tag, group, kept.pop((tag, group)).astype(bf16))

    run_heads(jobs, query_of, kt_ref, ve_ref, head_size, finish)


def pack_kernel(lanes, clusters, dest_ref, points_ref, *rest):
    packed = rest[:lanes]
    counts, sems = rest[lanes:]
    me = lax.axis_index("ball")
    for offset in range(lanes):
        counts[offset] = 0

    def copy(cluster, target, place):
        return pltpu.make_async_copy(
            points_ref.at[pl.ds(cluster * CLUSTER, CLUSTER)],
            target.at[pl.ds(place, CLUSTER)],
            sems.at[cluster],
        )

    for cluster in range(clusters):
        offset = owner_offset(dest_ref, cluster, clusters, lanes, me)
        rank = counts[offset]
        counts[offset] = rank + 1
        place = pl.multiple_of(rank * CLUSTER, CLUSTER)
        for which in range(lanes):

            @pl.when(offset == which)
            def _(cluster=cluster, which=which, place=place):
                copy(cluster, packed[which], place).start()

    for cluster in range(clusters):
        copy(cluster, packed[0], 0).wait()


def project_kernel(points_ref, gain_ref, wqk_ref, wv_ref, q_ref, k_ref, v_ref, pool_ref):
    rows, columns = points_ref.shape
    normed = rms_norm(points_ref[...], gain_ref[...])
    paired = dot32(normed, wqk_ref[...]).astype(bf16)
    values = dot32(normed, wv_ref[...]).astype(bf16)
    keys = paired[:, columns:]
    q_ref[...] = paired[:, :columns]
    k_ref[...] = keys
    v_ref[...] = values
    pooled = rows // POOL
    row = lax.broadcasted_iota(jnp.int32, (pooled, rows), 0)
    column = lax.broadcasted_iota(jnp.int32, (pooled, rows), 1)
    averaging = jnp.where(column // POOL == row, 1.0 / math.sqrt(POOL), 0.0).astype(bf16)
    pool_ref[:pooled] = dot32(averaging, keys).astype(bf16)
    pool_ref[pooled:] = dot32(averaging, values).astype(bf16)


def near_part_kernel(group, q_ref, k_ref, v_ref, o_ref, m_ref, l_ref, kt_ref, ve_ref):
    rows, columns = o_ref.shape[0], k_ref.shape[1]
    key_count = k_ref.shape[0]
    head_size = columns // HEADS
    per_tile = LANE_TILE // head_size
    tile = slice(group * LANE_TILE, (group + 1) * LANE_TILE)
    set_keys(kt_ref, 0, k_ref[:, tile])
    ve_ref[0, :, :LANE_TILE] = v_ref[:, tile]
    ve_ref[0, :, LANE_TILE:] = jnp.ones((key_count, LANE_TILE), bf16)
    kept = {}

    def finish(tag, head, mixed, total, row_max):
        for name, new in (("o", mixed), ("m", row_max), ("l", total)):
            kept[tag, name] = place_head(kept.get((tag, name)), head, per_tile, head_size, new)
        if head == per_tile - 1:
            block = pl.ds(tag, min(BLOCK, rows))
            o_ref[block] = kept.pop((tag, "o"))
            m_ref[block] = kept.pop((tag, "m"))
            l_ref[block] = kept.pop((tag, "l"))

    jobs = [
        (start, head, 0, key_count)
        for start in range(0, rows, BLOCK)
        for head in range(per_tile)
    ]
    run_heads(
        jobs,
        lambda start: q_ref[pl.ds(start, min(BLOCK, rows)), tile],
        kt_ref,
        ve_ref,
        head_size,
        finish,
    )


def near_kernel(parts, q_ref, k_ref, v_ref, pool_ref, *rest):
    partial = [rest[3 * part : 3 * part + 3] for part in range(parts)]
    out_ref, kt_ref, ve_ref = rest[3 * parts :]
    rows, columns = q_ref.shape
    local = k_ref.shape[0]
    regions = pool_ref.shape[0]
    pooled = pool_ref.shape[1] // 2
    total_keys = local + regions * pooled
    head_size = columns // HEADS
    per_tile = LANE_TILE // head_size
    early = partial[0][0].shape[0]
    factor = math.log2(math.e) / math.sqrt(head_size)
    set_keys(kt_ref, 0, k_ref[...])
    set_values(ve_ref, 0, v_ref[...])
    set_keys(kt_ref, local, jnp.concatenate([pool_ref[r, :pooled] for r in range(regions)], axis=0))
    set_values(
        ve_ref, local, jnp.concatenate([pool_ref[r, pooled:] for r in range(regions)], axis=0)
    )
    kept = {}

    def finish(tag, head, mixed, total, row_max):
        group = head // per_tile
        if tag < early:
            for name, new in (("o", mixed), ("m", row_max), ("l", total)):
                kept[tag, group, name] = place_head(
                    kept.get((tag, group, name)), head, per_tile, head_size, new
                )
        else:
            kept[tag, group, "o"] = place_head(
                kept.get((tag, group, "o")), head, per_tile, head_size, mixed / total
            )
        if head % per_tile < per_tile - 1:
            return
        block = pl.ds(tag, BLOCK)
        result = kept.pop((tag, group, "o"))
        if tag < early:
            o_ref, m_ref, l_ref = partial[group]
            new_max, new_total = kept.pop((tag, group, "m")), kept.pop((tag, group, "l"))
            old_max = m_ref[block]
            top = jnp.maximum(new_max, old_max)
            new_part = jnp.exp2((new_max - top) * factor)
            old_part = jnp.exp2((old_max - top) * factor)
            result = (result * new_part + o_ref[block] * old_part) / (
                new_total * new_part + l_ref[block] * old_part
            )
        out_ref[block, group * LANE_TILE : (group + 1) * LANE_TILE] = result.astype(bf16)

    jobs = [
        (start, head, local if start < early else 0, total_keys)
        for start in range(0, rows, BLOCK)
        for head in range(HEADS)
    ]
    run_heads(jobs, lambda start: q_ref[pl.ds(start, BLOCK)], kt_ref, ve_ref, head_size, finish)


def far_kernel(lanes, clusters, dest_ref, *rest):
    arrived = rest[:lanes]
    gain_ref, wqk_ref, wv_ref = rest[lanes : lanes + 3]
    leaving = rest[lanes + 3 : 2 * lanes + 3]
    x_ref, q_ref, y_ref, kt_ref, ve_ref, member, in_sems, out_sems = rest[2 * lanes + 3 :]
    rows, columns = x_ref.shape
    share = arrived[0].shape[0]
    me = lax.axis_index("ball")
    for offset in range(lanes):
        member[offset] = 0
    for cluster in range(clusters):
        member[owner_offset(dest_ref, cluster, clusters, lanes, me)] = 1
    places, place = [], 0
    for offset in range(lanes):
        places.append(pl.multiple_of(place * share, share))
        place = place + member[offset]

    def fetch(offset):
        return pltpu.make_async_copy(
            arrived[offset], x_ref.at[pl.ds(places[offset], share)], in_sems.at[offset]
        )

    def give(offset):
        return pltpu.make_async_copy(
            y_ref.at[pl.ds(places[offset], share)], leaving[offset], out_sems.at[offset]
        )

    def for_members(act):
        for offset in range(lanes):

            @pl.when(member[offset] == 1)
            def _(offset=offset):
                act(offset)

    for_members(lambda offset: fetch(offset).start())
    for_members(lambda offset: fetch(offset).wait())
    normed = rms_norm(x_ref[...], gain_ref[...])
    paired = dot32(normed, wqk_ref[...]).astype(bf16)
    q_ref[...] = paired[:, :columns]
    set_keys(kt_ref, 0, paired[:, columns:])
    set_values(ve_ref, 0, dot32(normed, wv_ref[...]).astype(bf16))

    def store(tag, group, result):
        y_ref[pl.ds(tag, BLOCK), group * LANE_TILE : (group + 1) * LANE_TILE] = result

    jobs = [(start, head, 0, rows) for start in range(0, rows, BLOCK) for head in range(HEADS)]
    full_attention(
        jobs, lambda start: q_ref[pl.ds(start, BLOCK)], kt_ref, ve_ref, columns, store
    )
    for_members(lambda offset: give(offset).start())
    for_members(lambda offset: give(offset).wait())


def finish_kernel(lanes, clusters, dest_ref, points_ref, near_ref, *rest):
    returned = rest[:lanes]
    wo_ref, gain_ref, up_ref, down_ref, out_ref, far_ref, counts, sems = rest[lanes:]
    me = lax.axis_index("ball")
    for offset in range(lanes):
        counts[offset] = 0

    def copy(cluster, source, place):
        return pltpu.make_async_copy(
            source.at[pl.ds(place, CLUSTER)],
            far_ref.at[pl.ds(cluster * CLUSTER, CLUSTER)],
            sems.at[cluster],
        )

    for cluster in range(clusters):
        offset = owner_offset(dest_ref, cluster, clusters, lanes, me)
        rank = counts[offset]
        counts[offset] = rank + 1
        place = pl.multiple_of(rank * CLUSTER, CLUSTER)
        for which in range(lanes):

            @pl.when(offset == which)
            def _(cluster=cluster, which=which, place=place):
                copy(cluster, returned[which], place).start()

    for cluster in range(clusters):
        copy(cluster, returned[0], 0).wait()
    rows = points_ref.shape[0]
    for start in range(0, rows, BLOCK):
        block = pl.ds(start, BLOCK)
        after = (
            points_ref[block].astype(f32)
            + dot32(near_ref[block], wo_ref[...])
            + dot32(far_ref[block], wo_ref[...])
        ).astype(bf16)
        normed = rms_norm(after, gain_ref[...])
        hidden = jax.nn.gelu(dot32(normed, up_ref[...]), approximate=True).astype(bf16)
        out_ref[block] = (after.astype(f32) + dot32(hidden, down_ref[...])).astype(bf16)


def per_device(
    points, gain_attn, w_query_key, w_value, w_out, gain_mlp, w_up, w_down, cluster_dest
):
    columns = points.shape[-1]
    flat = points.reshape(-1, columns)
    rows = flat.shape[0]
    lanes, regions = lax.axis_size("ball"), lax.axis_size("region")
    clusters = rows // CLUSTER
    share = 2 * clusters // lanes * CLUSTER
    pooled = rows // POOL
    dest = cluster_dest.reshape(clusters)
    gain_first = gain_attn.reshape(1, columns)
    gain_second = gain_mlp.reshape(1, columns)
    groups = columns // LANE_TILE
    early = rows // 2
    wide = jax.ShapeDtypeStruct((rows, columns), bf16)
    piece = jax.ShapeDtypeStruct((share, columns), bf16)

    def attention_cost(queries, keys, heads):
        return cost(4 * heads * queries * keys * 256, 4 * rows * columns, heads * queries * keys)

    def shift(data, offset):
        return lax.ppermute(data, "ball", [(i, (i + offset) % lanes) for i in range(lanes)])

    packed = pl.pallas_call(
        functools.partial(pack_kernel, lanes, clusters),
        out_shape=[piece] * lanes,
        in_specs=[in_smem(), anywhere()],
        out_specs=[anywhere()] * lanes,
        scratch_shapes=[
            pltpu.SMEM((lanes,), jnp.int32),
            pltpu.SemaphoreType.DMA((clusters,)),
        ],
        cost_estimate=cost(0, 4 * rows * columns),
        compiler_params=params(),
        name="pack",
    )(dest, flat)
    arrived = [packed[0]] + [shift(packed[d], d) for d in range(1, lanes)]

    query, keys, values, pool = pl.pallas_call(
        project_kernel,
        out_shape=[wide] * 3 + [jax.ShapeDtypeStruct((2 * pooled, columns), bf16)],
        in_specs=[in_vmem()] * 4,
        out_specs=[in_vmem()] * 4,
        cost_estimate=cost(6 * rows * columns * columns, 10 * rows * columns),
        compiler_params=params(),
        name="project",
    )(flat, gain_first, w_query_key, w_value)

    gathered = pool.reshape(1, 2 * pooled, columns)
    step = regions // 2
    while step:
        other = lax.ppermute(gathered, "region", [(i, i ^ step) for i in range(regions)])
        gathered = jnp.concatenate([gathered, other], axis=0)
        step //= 2

    partial = []
    for group in range(groups):
        partial += pl.pallas_call(
            functools.partial(near_part_kernel, group),
            out_shape=[jax.ShapeDtypeStruct((early, LANE_TILE), f32)] * 3,
            in_specs=[in_vmem()] * 3,
            out_specs=[in_vmem()] * 3,
            scratch_shapes=[
                pltpu.VMEM((LANE_TILE, rows), bf16),
                pltpu.VMEM((1, rows, 2 * LANE_TILE), bf16),
            ],
            cost_estimate=attention_cost(early, rows, HEADS // groups),
            compiler_params=params(),
            name="near_part",
        )(query, keys, values)

    leaving = pl.pallas_call(
        functools.partial(far_kernel, lanes, clusters),
        out_shape=[piece] * lanes,
        in_specs=[in_smem()] + [anywhere()] * lanes + [in_vmem()] * 3,
        out_specs=[anywhere()] * lanes,
        scratch_shapes=[
            pltpu.VMEM((rows, columns), bf16),
            pltpu.VMEM((rows, columns), bf16),
            pltpu.VMEM((rows, columns), bf16),
            pltpu.VMEM((columns, rows), bf16),
            pltpu.VMEM((groups, rows, 2 * LANE_TILE), bf16),
            pltpu.SMEM((lanes,), jnp.int32),
            pltpu.SemaphoreType.DMA((lanes,)),
            pltpu.SemaphoreType.DMA((lanes,)),
        ],
        cost_estimate=attention_cost(rows, rows, HEADS),
        compiler_params=params(),
        name="far",
    )(dest, *arrived, gain_first, w_query_key, w_value)
    returned = [leaving[0]] + [shift(leaving[d], lanes - d) for d in range(1, lanes)]

    near_keys = rows + regions * pooled
    near = pl.pallas_call(
        functools.partial(near_kernel, groups),
        out_shape=wide,
        in_specs=[in_vmem()] * (4 + 3 * groups),
        out_specs=in_vmem(),
        scratch_shapes=[
            pltpu.VMEM((columns, near_keys), bf16),
            pltpu.VMEM((groups, near_keys, 2 * LANE_TILE), bf16),
        ],
        cost_estimate=attention_cost(rows, near_keys - rows // 2, HEADS),
        compiler_params=params(),
        name="near",
    )(query, keys, values, gathered, *partial)

    block_out = pl.pallas_call(
        functools.partial(finish_kernel, lanes, clusters),
        out_shape=wide,
        in_specs=[in_smem()] + [in_vmem()] * 2 + [anywhere()] * lanes + [in_vmem()] * 4,
        out_specs=in_vmem(),
        scratch_shapes=[
            pltpu.VMEM((rows, columns), bf16),
            pltpu.SMEM((lanes,), jnp.int32),
            pltpu.SemaphoreType.DMA((clusters,)),
        ],
        cost_estimate=cost(20 * rows * columns * columns, 8 * rows * columns),
        compiler_params=params(),
        name="finish",
    )(dest, flat, near, *returned, w_out, gain_second, w_up, w_down)
    return block_out.reshape(points.shape)


def solution(mesh):
    placed = (
        P("ball", "region", None, None),
        P(),
        P(),
        P(),
        P(),
        P(),
        P(),
        P(),
        P("ball", "region", None),
    )
    return jax.shard_map(
        per_device,
        mesh=mesh,
        in_specs=placed,
        out_specs=P("ball", "region", None, None),
        check_vma=False,
    )
```

```python
import functools
import math

import jax
import jax.numpy as jnp
from jax import lax
from jax.experimental import pallas as pl
from jax.experimental.pallas import tpu as pltpu
from jax.sharding import PartitionSpec as P

HEADS = 8
CLUSTER = 64
POOL = 16
TILE = 128
SLOW_BLOCK = 256
SAFE_EXPONENT = 104.0
VMEM_LIMIT = 48 * 1024 * 1024

bf16 = jnp.bfloat16
f32 = jnp.float32


def in_vmem():
    return pl.BlockSpec(memory_space=pltpu.VMEM)


def in_smem():
    return pl.BlockSpec(memory_space=pltpu.SMEM)


def anywhere():
    return pl.BlockSpec(memory_space=pl.ANY)


def params():
    return pltpu.CompilerParams(vmem_limit_bytes=VMEM_LIMIT)


def cost(flops, moved, transcendentals=0):
    return pl.CostEstimate(
        flops=int(flops), bytes_accessed=int(moved), transcendentals=int(transcendentals)
    )


def rms_norm(rows, gain):
    widened = rows.astype(f32)
    scaling = lax.rsqrt(jnp.mean(widened * widened, axis=1, keepdims=True) + 1e-06)
    return (widened * scaling * gain).astype(bf16)


def dot32(left, right):
    return jnp.dot(left, right, preferred_element_type=f32)


def packed_places(dest_ref, clusters, lanes, slots, counts):
    me = lax.axis_index("ball")
    capacity = 2 * clusters // lanes
    offsets = []
    for offset in range(lanes):
        slots[offset] = 0
        counts[offset] = 0
    for cluster in range(clusters):
        offset = lax.rem(dest_ref[cluster] // clusters - me + lanes, lanes)
        slots[offset] = 1
        offsets.append(offset)
    if capacity * 2 == clusters:
        low, high = offsets[0], offsets[0]
        for offset in offsets[1:]:
            low, high = jnp.minimum(low, offset), jnp.maximum(high, offset)
        swap = high - low > lanes // 2
        slots[low] = jnp.where(swap, 1, 0)
        slots[high] = jnp.where(swap, 0, 1)
        across = high - low == lanes // 2
    else:
        taken = 0
        for offset in range(lanes):
            here = slots[offset]
            slots[offset] = taken
            taken = taken + here
        across = None
    places = []
    for offset in offsets:
        rank = counts[offset]
        counts[offset] = rank + 1
        place = (slots[offset] * capacity + rank) * CLUSTER
        places.append(pl.multiple_of(place, CLUSTER))
    return places, across


def factor_of(head_size):
    return math.log2(math.e) / math.sqrt(head_size)


def extended_values(values, head_size):
    columns, rows = values.shape[1], values.shape[0]
    turned = values.T
    ones = jnp.ones((16, rows), bf16)
    return [
        jnp.concatenate([turned[h * head_size : (h + 1) * head_size], ones], axis=0)
        for h in range(columns // head_size)
    ]


def masked_query(query, head, head_size):
    row = lax.broadcasted_iota(jnp.int32, (TILE, 1), 0) // head_size
    return jnp.where(row == head % (TILE // head_size), query, bf16(0))


def run_jobs(jobs, ahead=1):
    waiting = [scores() for scores, _ in jobs[:ahead]]
    for index, (_, finish) in enumerate(jobs):
        if index + ahead < len(jobs):
            waiting.append(jobs[index + ahead][0]())
        finish(waiting.pop(0))


def plain_weights(scores, head_size):
    return jnp.exp2(scores * factor_of(head_size)).astype(bf16)


def head_norms(rows, head_size):
    columns = rows.shape[1]
    widened = rows.astype(f32)
    channel = lax.broadcasted_iota(jnp.int32, (columns, TILE), 0) // head_size
    head = lax.broadcasted_iota(jnp.int32, (columns, TILE), 1)
    members = (channel == head).astype(bf16)
    return jnp.max(dot32((widened * widened).astype(bf16), members), axis=0, keepdims=True)


def exponents_safe(query_norms, key_norms, head_size):
    limit = (SAFE_EXPONENT / factor_of(head_size)) ** 2
    return jnp.max(query_norms * key_norms) <= limit


def shifted_attention(qt_ref, start, count, parts, head_size, out_ref):
    per_tile = TILE // head_size

    def step(index, carry):
        head = index % HEADS
        block = pl.multiple_of(start + index // HEADS * SLOW_BLOCK, SLOW_BLOCK)
        tile = pl.multiple_of(head // per_tile * TILE, TILE)
        query = masked_query(
            qt_ref[pl.ds(tile, TILE), pl.ds(block, SLOW_BLOCK)], head, head_size
        )
        loaded = [part(pl.ds(tile, TILE), head) for part in parts]
        scores = [dot32(keys, query) for keys, _ in loaded]
        top = jnp.max(scores[0], axis=0, keepdims=True)
        for more in scores[1:]:
            top = jnp.maximum(top, jnp.max(more, axis=0, keepdims=True))
        mixed = 0.0
        for block_scores, (_, values) in zip(scores, loaded):
            mixed = mixed + dot32(values, plain_weights(block_scores - top, head_size))
        rows = pl.ds(pl.multiple_of(head * head_size, head_size), head_size)
        out_ref[rows, pl.ds(block, SLOW_BLOCK)] = (
            mixed[:head_size] / mixed[head_size : head_size + 1]
        ).astype(bf16)
        return carry

    lax.fori_loop(0, HEADS * (count // SLOW_BLOCK), step, 0)


def pack_kernel(lanes, clusters, dest_ref, points_ref, packed_ref, slots, counts, sems):
    places, _ = packed_places(dest_ref, clusters, lanes, slots, counts)
    copies = [
        pltpu.make_async_copy(
            points_ref.at[pl.ds(cluster * CLUSTER, CLUSTER)],
            packed_ref.at[pl.ds(place, CLUSTER)],
            sems.at[cluster],
        )
        for cluster, place in enumerate(places)
    ]
    for copy in copies:
        copy.start()
    for copy in copies:
        copy.wait()


def project_kernel(
    head_size, points_ref, gain_ref, wqk_ref, wv_ref, qt_ref, k_ref, vt_ref, pool_ref, norms_ref
):
    rows, columns = points_ref.shape
    normed = rms_norm(points_ref[...], gain_ref[...])
    paired = dot32(normed, wqk_ref[...]).astype(bf16)
    values = dot32(normed, wv_ref[...]).astype(bf16)
    query, keys = paired[:, :columns], paired[:, columns:]
    k_ref[...] = keys
    pooled = rows // POOL
    row = lax.broadcasted_iota(jnp.int32, (pooled, rows), 0)
    column = lax.broadcasted_iota(jnp.int32, (pooled, rows), 1)
    averaging = jnp.where(column // POOL == row, 1.0 / math.sqrt(POOL), 0.0).astype(bf16)
    pool_ref[:pooled] = dot32(averaging, keys).astype(bf16)
    pool_ref[pooled:] = dot32(averaging, values).astype(bf16)
    qt_ref[...] = query.T
    for head, extended in enumerate(extended_values(values, head_size)):
        vt_ref[head] = extended
    norms_ref[0:1] = head_norms(query, head_size)
    norms_ref[1:2] = head_norms(keys, head_size)


def near_part_kernel(group, head_size, qt_ref, k_ref, vt_ref, o_ref):
    per_tile = TILE // head_size
    kept = o_ref.shape[1]
    tile = slice(group * TILE, (group + 1) * TILE)

    def job(inner):
        head = group * per_tile + inner

        def scores():
            return dot32(k_ref[:, tile], masked_query(qt_ref[tile, :], head, head_size))

        def finish(values):
            mixed = dot32(vt_ref[head], plain_weights(values, head_size))
            o_ref[inner] = mixed[:kept]

        return scores, finish

    run_jobs([job(inner) for inner in range(per_tile)])


def far_fast(head_size, qt_ref, k_ref, vt_ref, kr_ref, vr_ref, y_ref):
    half = k_ref.shape[0] // 2
    per_tile = TILE // head_size
    jobs = []
    sums = {}

    def job(side, head, own):
        tile = slice(head // per_tile * TILE, (head // per_tile + 1) * TILE)
        queries = slice(side * half, (side + 1) * half)
        rows = queries if own else slice((1 - side) * half, (2 - side) * half)
        key_ref, value_ref = (k_ref, vt_ref) if own else (kr_ref, vr_ref)

        def scores():
            query = masked_query(qt_ref[tile, queries], head, head_size)
            return dot32(key_ref[rows, tile], query)

        def finish(values):
            mixed = dot32(value_ref[head, :, rows], plain_weights(values, head_size))
            if own:
                sums[side, head] = mixed
                return
            mixed = mixed + sums.pop((side, head))
            y_ref[head * head_size : (head + 1) * head_size, queries] = (
                mixed[:head_size] / mixed[head_size : head_size + 1]
            ).astype(bf16)

        return scores, finish

    for side in range(2):
        for head in range(HEADS):
            for own in (True, False):
                jobs.append(job(side, head, own))
    run_jobs(jobs)


def far_kernel(
    lanes, clusters, head_size, dest_ref, next_ref, prior_ref, across_ref, qt_ref, k_ref, vt_ref,
    norms_ref, gain_ref, wqk_ref, wv_ref, out_ref, x_ref, kr_ref, vr_ref, y_ref, slots, counts,
    sems,
):
    rows, columns = x_ref.shape
    half = rows // 2
    _, across = packed_places(dest_ref, clusters, lanes, slots, counts)

    def whole():
        return pltpu.make_async_copy(across_ref, x_ref, sems.at[0])

    def first():
        return pltpu.make_async_copy(next_ref, x_ref.at[pl.ds(0, half)], sems.at[0])

    def second():
        return pltpu.make_async_copy(prior_ref, x_ref.at[pl.ds(half, half)], sems.at[1])

    @pl.when(across)
    def _():
        whole().start()
        whole().wait()

    @pl.when(jnp.logical_not(across))
    def _():
        first().start()
        second().start()
        first().wait()
        second().wait()

    normed = rms_norm(x_ref[...], gain_ref[...])
    keys = dot32(normed, wqk_ref[:, columns:]).astype(bf16)
    values = dot32(normed, wv_ref[...]).astype(bf16)
    kr_ref[...] = keys
    for head, extended in enumerate(extended_values(values, head_size)):
        vr_ref[head] = extended
    key_norms = jnp.maximum(norms_ref[1:2], head_norms(keys, head_size))
    safe = exponents_safe(norms_ref[0:1], key_norms, head_size)

    @pl.when(safe)
    def _():
        far_fast(head_size, qt_ref, k_ref, vt_ref, kr_ref, vr_ref, y_ref)

    @pl.when(jnp.logical_not(safe))
    def _():
        for side in range(2):
            mine = slice(side * half, (side + 1) * half)
            other = slice((1 - side) * half, (2 - side) * half)
            shifted_attention(
                qt_ref,
                side * half,
                half,
                [
                    lambda tile, head, mine=mine: (k_ref[mine, tile], vt_ref[head, :, mine]),
                    lambda tile, head, other=other: (kr_ref[other, tile], vr_ref[head, :, other]),
                ],
                head_size,
                y_ref,
            )

    out_ref[...] = y_ref[...].T


def finish_kernel(
    lanes, clusters, head_size, groups, dest_ref, points_ref, far_ref, qt_ref, k_ref, vt_ref,
    norms_ref, pool_ref, *rest
):
    partial = rest[:groups]
    (wo_ref, gain_ref, up_ref, down_ref, out_ref, kp_ref, vp_ref, y_ref, done_ref, slots, counts,
     sems) = rest[groups:]
    rows, columns = points_ref.shape
    per_tile = TILE // head_size
    kept = partial[0].shape[1]
    regions, pooled = pool_ref.shape[0], pool_ref.shape[1] // 2
    for region in range(regions):
        kp_ref[region * pooled : (region + 1) * pooled] = pool_ref[region, :pooled]
    gathered = jnp.concatenate([pool_ref[r, pooled:] for r in range(regions)], axis=0)
    for head, extended in enumerate(extended_values(gathered, head_size)):
        vp_ref[head] = extended
    key_norms = jnp.maximum(norms_ref[1:2], head_norms(kp_ref[...], head_size))
    safe = exponents_safe(norms_ref[0:1], key_norms, head_size)

    def job(head):
        tile = slice(head // per_tile * TILE, (head // per_tile + 1) * TILE)

        def scores():
            return dot32(kp_ref[:, tile], masked_query(qt_ref[tile, :], head, head_size))

        def finish(values):
            mixed = dot32(vp_ref[head], plain_weights(values, head_size))[:kept]
            mixed = mixed + partial[head // per_tile][head % per_tile]
            y_ref[head * head_size : (head + 1) * head_size, :] = (
                mixed[:head_size] / mixed[head_size : head_size + 1]
            ).astype(bf16)

        return scores, finish

    @pl.when(safe)
    def _():
        run_jobs([job(head) for head in range(HEADS)])

    @pl.when(jnp.logical_not(safe))
    def _():
        shifted_attention(
            qt_ref,
            0,
            rows,
            [
                lambda tile, head: (k_ref[:, tile], vt_ref[head]),
                lambda tile, head: (kp_ref[:, tile], vp_ref[head]),
            ],
            head_size,
            y_ref,
        )

    step = min(rows, 512)
    for start in range(0, rows, step):
        block = slice(start, start + step)
        after = (
            points_ref[block].astype(f32)
            + dot32(y_ref[:, block].T, wo_ref[...])
            + dot32(far_ref[block], wo_ref[...])
        ).astype(bf16)
        normed = rms_norm(after, gain_ref[...])
        hidden = jax.nn.gelu(dot32(normed, up_ref[...]), approximate=True).astype(bf16)
        done_ref[block] = (after.astype(f32) + dot32(hidden, down_ref[...])).astype(bf16)
    places, _ = packed_places(dest_ref, clusters, lanes, slots, counts)
    copies = [
        pltpu.make_async_copy(
            done_ref.at[pl.ds(place, CLUSTER)],
            out_ref.at[pl.ds(cluster * CLUSTER, CLUSTER)],
            sems.at[cluster],
        )
        for cluster, place in enumerate(places)
    ]
    for copy in copies:
        copy.start()
    for copy in copies:
        copy.wait()


def owner_far_kernel(head_size, x_ref, gain_ref, wqk_ref, wv_ref, out_ref, qt, k, vt, y):
    rows, columns = x_ref.shape
    normed = rms_norm(x_ref[...], gain_ref[...])
    paired = dot32(normed, wqk_ref[...]).astype(bf16)
    values = dot32(normed, wv_ref[...]).astype(bf16)
    qt[...] = paired[:, :columns].T
    k[...] = paired[:, columns:]
    for head, extended in enumerate(extended_values(values, head_size)):
        vt[head] = extended
    shifted_attention(
        qt, 0, rows, [lambda tile, head: (k[:, tile], vt[head])], head_size, y
    )
    out_ref[...] = y[...].T


def per_device(
    points, gain_attn, w_query_key, w_value, w_out, gain_mlp, w_up, w_down, cluster_dest
):
    columns = points.shape[-1]
    flat = points.reshape(-1, columns)
    rows = flat.shape[0]
    lanes, regions = lax.axis_size("ball"), lax.axis_size("region")
    clusters = rows // CLUSTER
    share = 2 * clusters // lanes * CLUSTER
    owners = rows // share
    pooled = rows // POOL
    head_size = columns // HEADS
    tall = head_size + 16
    kept = head_size + 8
    dest = cluster_dest.reshape(clusters)
    gain_first = gain_attn.reshape(1, columns)
    gain_second = gain_mlp.reshape(1, columns)
    groups = columns // TILE
    wide = jax.ShapeDtypeStruct((rows, columns), bf16)
    turned = jax.ShapeDtypeStruct((columns, rows), bf16)
    extended = jax.ShapeDtypeStruct((HEADS, tall, rows), bf16)
    scalars = [pltpu.SMEM((lanes,), jnp.int32)] * 2

    def attention_cost(queries, keys, heads):
        return cost(3 * heads * queries * keys * 256, 4 * rows * columns, heads * queries * keys)

    def shift(data, offset):
        return lax.ppermute(data, "ball", [(i, (i + offset) % lanes) for i in range(lanes)])

    packed = pl.pallas_call(
        functools.partial(pack_kernel, lanes, clusters),
        out_shape=wide,
        in_specs=[in_smem(), anywhere()],
        out_specs=anywhere(),
        scratch_shapes=scalars + [pltpu.SemaphoreType.DMA((clusters,))],
        cost_estimate=cost(0, 4 * rows * columns),
        compiler_params=params(),
        name="pack",
    )(dest, flat)

    pair_path = owners == 2 and lanes == 4
    if pair_path:
        from_next = shift(packed[:share], lanes - 1)
        from_prior = shift(packed[share:], 1)
        from_across = shift(packed, 2)

    query, keys, values, pool, norms = pl.pallas_call(
        functools.partial(project_kernel, head_size),
        out_shape=[
            turned,
            wide,
            extended,
            jax.ShapeDtypeStruct((2 * pooled, columns), bf16),
            jax.ShapeDtypeStruct((8, TILE), f32),
        ],
        in_specs=[in_vmem()] * 4,
        out_specs=[in_vmem()] * 5,
        cost_estimate=cost(6 * rows * columns * columns, 10 * rows * columns),
        compiler_params=params(),
        name="project",
    )(packed, gain_first, w_query_key, w_value)

    gathered = pool.reshape(1, 2 * pooled, columns)
    step = regions // 2
    while step:
        other = lax.ppermute(gathered, "region", [(i, i ^ step) for i in range(regions)])
        gathered = jnp.concatenate([gathered, other], axis=0)
        step //= 2

    partial = [
        pl.pallas_call(
            functools.partial(near_part_kernel, group, head_size),
            out_shape=jax.ShapeDtypeStruct((HEADS // groups, kept, rows), f32),
            in_specs=[in_vmem()] * 3,
            out_specs=in_vmem(),
            cost_estimate=attention_cost(rows, rows, HEADS // groups),
            compiler_params=params(),
            name="near_part",
        )(query, keys, values)
        for group in range(groups)
    ]

    if pair_path:
        far = pl.pallas_call(
            functools.partial(far_kernel, lanes, clusters, head_size),
            out_shape=wide,
            in_specs=[in_smem()] + [anywhere()] * 3 + [in_vmem()] * 7,
            out_specs=in_vmem(),
            scratch_shapes=[
                pltpu.VMEM((rows, columns), bf16),
                pltpu.VMEM((rows, columns), bf16),
                pltpu.VMEM((HEADS, tall, rows), bf16),
                pltpu.VMEM((columns, rows), bf16),
            ]
            + scalars
            + [pltpu.SemaphoreType.DMA((2,))],
            cost_estimate=attention_cost(rows, rows, HEADS),
            compiler_params=params(),
            name="far",
        )(
            dest, from_next, from_prior, from_across, query, keys, values, norms, gain_first,
            w_query_key, w_value,
        )
    else:
        targets = dest // clusters
        members = lax.rem(targets - lax.axis_index("ball") + lanes, lanes)
        present = jnp.zeros((lanes,), jnp.int32).at[members].set(1)
        slot = jnp.cumsum(present) - present
        blocks = packed.reshape(owners, share, columns)
        empty = jnp.zeros((owners, share, columns), bf16)
        arrived, back = empty, empty

        def picked(source, offset):
            return lax.dynamic_index_in_dim(source, jnp.minimum(slot[offset], owners - 1), 0, False)

        def put(target, offset, block):
            index = jnp.minimum(slot[offset], owners - 1)
            placed = lax.dynamic_update_index_in_dim(target, block, index, 0)
            return jnp.where(present[offset] == 1, placed, target)

        for offset in range(lanes):
            block = picked(blocks, offset)
            arrived = put(arrived, offset, shift(block, offset) if offset else block)
        far_rotated = pl.pallas_call(
            functools.partial(owner_far_kernel, head_size),
            out_shape=wide,
            in_specs=[in_vmem()] * 4,
            out_specs=in_vmem(),
            scratch_shapes=[
                pltpu.VMEM((columns, rows), bf16),
                pltpu.VMEM((rows, columns), bf16),
                pltpu.VMEM((HEADS, tall, rows), bf16),
                pltpu.VMEM((columns, rows), bf16),
            ],
            cost_estimate=attention_cost(rows, rows, HEADS),
            compiler_params=params(),
            name="owner_far",
        )(arrived.reshape(rows, columns), gain_first, w_query_key, w_value)
        leaving = far_rotated.reshape(owners, share, columns)
        for offset in range(lanes):
            block = picked(leaving, offset)
            back = put(back, offset, shift(block, lanes - offset) if offset else block)
        far = back.reshape(rows, columns)

    block_out = pl.pallas_call(
        functools.partial(finish_kernel, lanes, clusters, head_size, groups),
        out_shape=wide,
        in_specs=[in_smem()] + [in_vmem()] * (7 + groups + 4),
        out_specs=anywhere(),
        scratch_shapes=[
            pltpu.VMEM((regions * pooled, columns), bf16),
            pltpu.VMEM((HEADS, tall, regions * pooled), bf16),
            pltpu.VMEM((columns, rows), bf16),
            pltpu.VMEM((rows, columns), bf16),
        ]
        + scalars
        + [pltpu.SemaphoreType.DMA((clusters,))],
        cost_estimate=cost(20 * rows * columns * columns, 8 * rows * columns),
        compiler_params=params(),
        name="finish",
    )(
        dest, packed, far, query, keys, values, norms, gathered, *partial, w_out, gain_second,
        w_up, w_down,
    )
    return block_out.reshape(points.shape)


def solution(mesh):
    placed = (
        P("ball", "region", None, None),
        P(),
        P(),
        P(),
        P(),
        P(),
        P(),
        P(),
        P("ball", "region", None),
    )
    return jax.shard_map(
        per_device,
        mesh=mesh,
        in_specs=placed,
        out_specs=P("ball", "region", None, None),
        check_vma=False,
    )
```

```python
import functools
import math

import jax
import jax.numpy as jnp
from jax import lax
from jax.experimental import pallas as pl
from jax.experimental.pallas import tpu as pltpu
from jax.sharding import PartitionSpec as P

HEADS = 8
CLUSTER = 64
POOL = 16
TILE = 128
SLOW_BLOCK = 256
QUERY_BLOCK = 512
KEY_BLOCK = 256
AHEAD = 3
ROW_BLOCK = 256
SAFE_EXPONENT = 104.0
VMEM_LIMIT = 48 * 1024 * 1024

bf16 = jnp.bfloat16
f32 = jnp.float32


def in_vmem():
    return pl.BlockSpec(memory_space=pltpu.VMEM)


def in_smem():
    return pl.BlockSpec(memory_space=pltpu.SMEM)


def in_hbm():
    return pl.BlockSpec(memory_space=pltpu.HBM)


def anywhere():
    return pl.BlockSpec(memory_space=pl.ANY)


def params():
    return pltpu.CompilerParams(vmem_limit_bytes=VMEM_LIMIT)


def cost(flops, moved, transcendentals=0):
    return pl.CostEstimate(
        flops=int(flops), bytes_accessed=int(moved), transcendentals=int(transcendentals)
    )


def rms_norm(rows, gain):
    widened = rows.astype(f32)
    scaling = lax.rsqrt(jnp.mean(widened * widened, axis=1, keepdims=True) + 1e-06)
    return (widened * scaling * gain).astype(bf16)


def dot32(left, right):
    return jnp.dot(left, right, preferred_element_type=f32)


def packed_places(dest_ref, clusters, lanes, slots, counts):
    me = lax.axis_index("ball")
    capacity = 2 * clusters // lanes
    offsets = []
    for offset in range(lanes):
        slots[offset] = 0
        counts[offset] = 0
    for cluster in range(clusters):
        offset = lax.rem(dest_ref[cluster] // clusters - me + lanes, lanes)
        slots[offset] = 1
        offsets.append(offset)
    if capacity * 2 == clusters:
        low, high = offsets[0], offsets[0]
        for offset in offsets[1:]:
            low, high = jnp.minimum(low, offset), jnp.maximum(high, offset)
        swap = high - low > lanes // 2
        slots[low] = jnp.where(swap, 1, 0)
        slots[high] = jnp.where(swap, 0, 1)
        across = high - low == lanes // 2
    else:
        taken = 0
        for offset in range(lanes):
            here = slots[offset]
            slots[offset] = taken
            taken = taken + here
        across = None
    places = []
    for offset in offsets:
        rank = counts[offset]
        counts[offset] = rank + 1
        place = (slots[offset] * capacity + rank) * CLUSTER
        places.append(pl.multiple_of(place, CLUSTER))
    return places, across


def factor_of(head_size):
    return math.log2(math.e) / math.sqrt(head_size)


def extended_values(values, head_size):
    columns, rows = values.shape[1], values.shape[0]
    turned = values.T
    ones = jnp.ones((16, rows), bf16)
    return [
        jnp.concatenate([turned[h * head_size : (h + 1) * head_size], ones], axis=0)
        for h in range(columns // head_size)
    ]


def masked_query(query, head, head_size):
    row = lax.broadcasted_iota(jnp.int32, (TILE, 1), 0) // head_size
    return jnp.where(row == head % (TILE // head_size), query, bf16(0))


def run_jobs(jobs, ahead=AHEAD):
    waiting = [first() for first, _ in jobs[:ahead]]
    for index, (_, second) in enumerate(jobs):
        if index + ahead < len(jobs):
            waiting.append(jobs[index + ahead][0]())
        second(waiting.pop(0))


def plain_weights(scores, head_size):
    return jnp.exp2(scores * factor_of(head_size)).astype(bf16)


def plain_attention(qt_ref, columns_of_query, heads, parts_of, head_size, store):
    per_tile = TILE // head_size
    kept = head_size + 8
    sums = {}
    jobs = []

    def job(start, head, key_ref, value_ref, first, last):
        tile = slice(head // per_tile * TILE, (head // per_tile + 1) * TILE)
        queries = slice(start, start + QUERY_BLOCK)
        rows = slice(first, first + KEY_BLOCK)

        def scores():
            query = masked_query(qt_ref[tile, queries], head, head_size)
            return dot32(key_ref[rows, tile], query)

        def mix(values):
            mixed = dot32(value_ref[head, :, rows], plain_weights(values, head_size))[:kept]
            if (start, head) in sums:
                mixed = mixed + sums.pop((start, head))
            if last:
                store(head, queries, mixed)
            else:
                sums[start, head] = mixed

        return scores, mix

    for start in columns_of_query:
        for head in heads:
            blocks = [
                (keys, values, row)
                for keys, values, first, end in parts_of(start)
                for row in range(first, end, KEY_BLOCK)
            ]
            for index, (keys, values, row) in enumerate(blocks):
                jobs.append(job(start, head, keys, values, row, index + 1 == len(blocks)))
    run_jobs(jobs)


def divided(sums, head_size):
    return (sums[:head_size] / sums[head_size : head_size + 1]).astype(bf16)


def head_norms(rows, head_size):
    columns = rows.shape[1]
    widened = rows.astype(f32)
    channel = lax.broadcasted_iota(jnp.int32, (columns, TILE), 0) // head_size
    head = lax.broadcasted_iota(jnp.int32, (columns, TILE), 1)
    members = (channel == head).astype(bf16)
    return jnp.max(dot32((widened * widened).astype(bf16), members), axis=0, keepdims=True)


def exponents_safe(query_norms, key_norms, head_size):
    limit = (SAFE_EXPONENT / factor_of(head_size)) ** 2
    return jnp.max(query_norms * key_norms) <= limit


def shifted_attention(qt_ref, start, count, parts, head_size, out_ref):
    per_tile = TILE // head_size

    def step(index, carry):
        head = index % HEADS
        block = pl.multiple_of(start + index // HEADS * SLOW_BLOCK, SLOW_BLOCK)
        tile = pl.multiple_of(head // per_tile * TILE, TILE)
        query = masked_query(
            qt_ref[pl.ds(tile, TILE), pl.ds(block, SLOW_BLOCK)], head, head_size
        )
        loaded = [part(pl.ds(tile, TILE), head) for part in parts]
        scores = [dot32(keys, query) for keys, _ in loaded]
        top = jnp.max(scores[0], axis=0, keepdims=True)
        for more in scores[1:]:
            top = jnp.maximum(top, jnp.max(more, axis=0, keepdims=True))
        mixed = 0.0
        for block_scores, (_, values) in zip(scores, loaded):
            mixed = mixed + dot32(values, plain_weights(block_scores - top, head_size))
        rows = pl.ds(pl.multiple_of(head * head_size, head_size), head_size)
        out_ref[rows, pl.ds(block, SLOW_BLOCK)] = (
            mixed[:head_size] / mixed[head_size : head_size + 1]
        ).astype(bf16)
        return carry

    lax.fori_loop(0, HEADS * (count // SLOW_BLOCK), step, 0)


def gelu(value):
    slope = math.sqrt(2.0 / math.pi)
    inner = value * (value * value * (0.044715 * slope) + slope)
    half = 0.5 * value
    return half + half * jnp.tanh(inner)


def pack_kernel(lanes, clusters, dest_hbm, points_ref, packed_ref, dest, slots, counts, sems):
    fetch = pltpu.make_async_copy(dest_hbm, dest, sems.at[clusters])
    fetch.start()
    fetch.wait()
    places, _ = packed_places(dest, clusters, lanes, slots, counts)
    copies = [
        pltpu.make_async_copy(
            points_ref.at[pl.ds(cluster * CLUSTER, CLUSTER)],
            packed_ref.at[pl.ds(place, CLUSTER)],
            sems.at[cluster],
        )
        for cluster, place in enumerate(places)
    ]
    for copy in copies:
        copy.start()
    for copy in copies:
        copy.wait()


def project_kernel(
    head_size, points_ref, gain_ref, wqk_ref, wv_ref, qt_ref, k_ref, vt_ref, pool_ref, norms_ref
):
    rows, columns = points_ref.shape
    normed = rms_norm(points_ref[...], gain_ref[...])
    paired = dot32(normed, wqk_ref[...]).astype(bf16)
    values = dot32(normed, wv_ref[...]).astype(bf16)
    query, keys = paired[:, :columns], paired[:, columns:]
    k_ref[...] = keys
    pooled = rows // POOL
    row = lax.broadcasted_iota(jnp.int32, (pooled, rows), 0)
    column = lax.broadcasted_iota(jnp.int32, (pooled, rows), 1)
    averaging = jnp.where(column // POOL == row, 1.0 / math.sqrt(POOL), 0.0).astype(bf16)
    pool_ref[:pooled] = dot32(averaging, keys).astype(bf16)
    pool_ref[pooled:] = dot32(averaging, values).astype(bf16)
    qt_ref[...] = query.T
    for head, extended in enumerate(extended_values(values, head_size)):
        vt_ref[head] = extended
    norms_ref[0:1] = head_norms(query, head_size)
    norms_ref[1:2] = head_norms(keys, head_size)


def near_part_kernel(group, head_size, qt_ref, k_ref, vt_ref, o_ref):
    per_tile = TILE // head_size
    rows = k_ref.shape[0]

    def store(head, queries, sums):
        o_ref[head % per_tile, :, queries] = sums

    plain_attention(
        qt_ref,
        range(0, rows, QUERY_BLOCK),
        range(group * per_tile, (group + 1) * per_tile),
        lambda start: [(k_ref, vt_ref, 0, rows)],
        head_size,
        store,
    )


def near_kernel(head_size, qt_ref, k_ref, vt_ref, norms_ref, pool_ref, *rest):
    partial = rest[:-3]
    y_ref, kp_ref, vp_ref = rest[-3:]
    rows = k_ref.shape[0]
    per_tile = TILE // head_size
    regions, pooled = pool_ref.shape[0], pool_ref.shape[1] // 2
    for region in range(regions):
        kp_ref[region * pooled : (region + 1) * pooled] = pool_ref[region, :pooled]
    gathered = jnp.concatenate([pool_ref[r, pooled:] for r in range(regions)], axis=0)
    for head, extended in enumerate(extended_values(gathered, head_size)):
        vp_ref[head] = extended
    key_norms = jnp.maximum(norms_ref[1:2], head_norms(kp_ref[...], head_size))
    safe = exponents_safe(norms_ref[0:1], key_norms, head_size)

    def store(head, queries, sums):
        sums = sums + partial[head // per_tile][head % per_tile, :, queries]
        y_ref[head * head_size : (head + 1) * head_size, queries] = divided(sums, head_size)

    @pl.when(safe)
    def _():
        plain_attention(
            qt_ref,
            range(0, rows, QUERY_BLOCK),
            range(HEADS),
            lambda start: [(kp_ref, vp_ref, 0, regions * pooled)],
            head_size,
            store,
        )

    @pl.when(jnp.logical_not(safe))
    def _():
        shifted_attention(
            qt_ref,
            0,
            rows,
            [
                lambda tile, head: (k_ref[:, tile], vt_ref[head]),
                lambda tile, head: (kp_ref[:, tile], vp_ref[head]),
            ],
            head_size,
            y_ref,
        )


def far_attention(
    head_size, across, next_ref, prior_ref, across_ref, qt_ref, k_ref, vt_ref, norms_ref,
    gain_ref, wqk_ref, wv_ref, kr_ref, vr_ref, y_ref,
):
    rows, columns = k_ref.shape
    half = rows // 2
    apart = jnp.concatenate([next_ref[...], prior_ref[...]], axis=0)
    normed = rms_norm(jnp.where(across, across_ref[...], apart), gain_ref[...])
    keys = dot32(normed, wqk_ref[:, columns:]).astype(bf16)
    values = dot32(normed, wv_ref[...]).astype(bf16)
    kr_ref[...] = keys
    for head, extended in enumerate(extended_values(values, head_size)):
        vr_ref[head] = extended
    key_norms = jnp.maximum(norms_ref[1:2], head_norms(keys, head_size))
    safe = exponents_safe(norms_ref[0:1], key_norms, head_size)

    def store(head, queries, sums):
        y_ref[head * head_size : (head + 1) * head_size, queries] = divided(sums, head_size)

    def parts_of(start):
        mine = start // half * half
        other = half - mine
        return [(k_ref, vt_ref, mine, mine + half), (kr_ref, vr_ref, other, other + half)]

    @pl.when(safe)
    def _():
        plain_attention(
            qt_ref, range(0, rows, QUERY_BLOCK), range(HEADS), parts_of, head_size, store
        )

    @pl.when(jnp.logical_not(safe))
    def _():
        for start in (0, half):
            mine, other = slice(start, start + half), slice(half - start, rows - start)
            shifted_attention(
                qt_ref,
                start,
                half,
                [
                    lambda tile, head, mine=mine: (k_ref[mine, tile], vt_ref[head, :, mine]),
                    lambda tile, head, other=other: (kr_ref[other, tile], vr_ref[head, :, other]),
                ],
                head_size,
                y_ref,
            )


def output_rows(
    places, points_ref, near_ref, far_ref, wo_ref, gain_ref, up_ref, down_ref, out_ref, done_ref,
    origin, sems,
):
    rows = points_ref.shape[0]
    for cluster, place in enumerate(places):
        origin[place // CLUSTER] = cluster

    def back(slot):
        return pltpu.make_async_copy(
            done_ref.at[pl.ds(slot * CLUSTER, CLUSTER)],
            out_ref.at[pl.ds(pl.multiple_of(origin[slot] * CLUSTER, CLUSTER), CLUSTER)],
            sems.at[slot],
        )

    def job(start):
        block = slice(start, start + ROW_BLOCK)

        def widen():
            after = (
                points_ref[block].astype(f32)
                + dot32(near_ref[:, block].T, wo_ref[...])
                + dot32(far_ref[:, block].T, wo_ref[...])
            ).astype(bf16)
            return after, dot32(rms_norm(after, gain_ref[...]), up_ref[...])

        def narrow(widened):
            after, hidden = widened
            hidden = gelu(hidden).astype(bf16)
            done_ref[block] = (after.astype(f32) + dot32(hidden, down_ref[...])).astype(bf16)
            for slot in range(start // CLUSTER, (start + ROW_BLOCK) // CLUSTER):
                back(slot).start()

        return widen, narrow

    run_jobs([job(start) for start in range(0, rows, ROW_BLOCK)], ahead=1)
    for slot in range(rows // CLUSTER):
        back(slot).wait()


def far_finish_kernel(
    lanes, clusters, head_size, dest_ref, points_ref, near_ref, next_ref, prior_ref, across_ref,
    qt_ref, k_ref, vt_ref, norms_ref, gain_ref, wqk_ref, wv_ref, wo_ref, gain_second, up_ref,
    down_ref, out_ref, kr_ref, vr_ref, y_ref, done_ref, slots, counts, origin, sems,
):
    places, across = packed_places(dest_ref, clusters, lanes, slots, counts)
    far_attention(
        head_size, across, next_ref, prior_ref, across_ref, qt_ref, k_ref, vt_ref, norms_ref,
        gain_ref, wqk_ref, wv_ref, kr_ref, vr_ref, y_ref,
    )
    output_rows(
        places, points_ref, near_ref, y_ref, wo_ref, gain_second, up_ref, down_ref, out_ref,
        done_ref, origin, sems,
    )


def finish_kernel(
    lanes, clusters, dest_ref, points_ref, near_ref, far_ref, wo_ref, gain_ref, up_ref, down_ref,
    out_ref, done_ref, slots, counts, origin, sems,
):
    places, _ = packed_places(dest_ref, clusters, lanes, slots, counts)
    output_rows(
        places, points_ref, near_ref, far_ref, wo_ref, gain_ref, up_ref, down_ref, out_ref,
        done_ref, origin, sems,
    )


def owner_far_kernel(head_size, x_ref, gain_ref, wqk_ref, wv_ref, out_ref, qt, k, vt, y):
    rows, columns = x_ref.shape
    normed = rms_norm(x_ref[...], gain_ref[...])
    paired = dot32(normed, wqk_ref[...]).astype(bf16)
    values = dot32(normed, wv_ref[...]).astype(bf16)
    qt[...] = paired[:, :columns].T
    k[...] = paired[:, columns:]
    for head, extended in enumerate(extended_values(values, head_size)):
        vt[head] = extended
    shifted_attention(
        qt, 0, rows, [lambda tile, head: (k[:, tile], vt[head])], head_size, y
    )
    out_ref[...] = y[...].T


def per_device(
    points, gain_attn, w_query_key, w_value, w_out, gain_mlp, w_up, w_down, cluster_dest
):
    columns = points.shape[-1]
    flat = points.reshape(-1, columns)
    rows = flat.shape[0]
    lanes, regions = lax.axis_size("ball"), lax.axis_size("region")
    clusters = rows // CLUSTER
    share = 2 * clusters // lanes * CLUSTER
    owners = rows // share
    pooled = rows // POOL
    head_size = columns // HEADS
    tall = head_size + 16
    kept = head_size + 8
    dest = cluster_dest.reshape(clusters)
    gain_first = gain_attn.reshape(1, columns)
    gain_second = gain_mlp.reshape(1, columns)
    groups = columns // TILE
    wide = jax.ShapeDtypeStruct((rows, columns), bf16)
    turned = jax.ShapeDtypeStruct((columns, rows), bf16)
    extended = jax.ShapeDtypeStruct((HEADS, tall, rows), bf16)
    scalars = [pltpu.SMEM((lanes,), jnp.int32)] * 2

    def attention_cost(queries, keys, heads):
        return cost(3 * heads * queries * keys * 256, 4 * rows * columns, heads * queries * keys)

    def shift(data, offset):
        return lax.ppermute(data, "ball", [(i, (i + offset) % lanes) for i in range(lanes)])

    packed = pl.pallas_call(
        functools.partial(pack_kernel, lanes, clusters),
        out_shape=wide,
        in_specs=[in_hbm(), in_hbm()],
        out_specs=anywhere(),
        scratch_shapes=[pltpu.SMEM((clusters,), jnp.int32)]
        + scalars
        + [pltpu.SemaphoreType.DMA((clusters + 1,))],
        cost_estimate=cost(0, 4 * rows * columns),
        compiler_params=params(),
        name="pack",
    )(dest, flat)

    pair_path = owners == 2 and lanes == 4
    if pair_path:
        from_next = shift(packed[:share], lanes - 1)
        from_prior = shift(packed[share:], 1)
        from_across = shift(packed, 2)

    query, keys, values, pool, norms = pl.pallas_call(
        functools.partial(project_kernel, head_size),
        out_shape=[
            turned,
            wide,
            extended,
            jax.ShapeDtypeStruct((2 * pooled, columns), bf16),
            jax.ShapeDtypeStruct((8, TILE), f32),
        ],
        in_specs=[in_vmem()] * 4,
        out_specs=[in_vmem()] * 5,
        cost_estimate=cost(6 * rows * columns * columns, 10 * rows * columns),
        compiler_params=params(),
        name="project",
    )(packed, gain_first, w_query_key, w_value)

    gathered = pool.reshape(1, 2 * pooled, columns)
    step = regions // 2
    while step:
        other = lax.ppermute(gathered, "region", [(i, i ^ step) for i in range(regions)])
        gathered = jnp.concatenate([gathered, other], axis=0)
        step //= 2

    partial = [
        pl.pallas_call(
            functools.partial(near_part_kernel, group, head_size),
            out_shape=jax.ShapeDtypeStruct((HEADS // groups, kept, rows), f32),
            in_specs=[in_vmem()] * 3,
            out_specs=in_vmem(),
            cost_estimate=attention_cost(rows, rows, HEADS // groups),
            compiler_params=params(),
            name="near_part",
        )(query, keys, values)
        for group in range(groups)
    ]

    near = pl.pallas_call(
        functools.partial(near_kernel, head_size),
        out_shape=turned,
        in_specs=[in_vmem()] * (5 + groups),
        out_specs=in_vmem(),
        scratch_shapes=[
            pltpu.VMEM((regions * pooled, columns), bf16),
            pltpu.VMEM((HEADS, tall, regions * pooled), bf16),
        ],
        cost_estimate=attention_cost(rows, regions * pooled, HEADS),
        compiler_params=params(),
        name="near",
    )(query, keys, values, norms, gathered, *partial)

    last_scratch = (
        [pltpu.VMEM((rows, columns), bf16)]
        + scalars
        + [pltpu.SMEM((clusters,), jnp.int32), pltpu.SemaphoreType.DMA((clusters,))]
    )
    if pair_path:
        block_out = pl.pallas_call(
            functools.partial(far_finish_kernel, lanes, clusters, head_size),
            out_shape=wide,
            in_specs=[in_smem()] + [in_vmem()] * 16,
            out_specs=anywhere(),
            scratch_shapes=[
                pltpu.VMEM((rows, columns), bf16),
                pltpu.VMEM((HEADS, tall, rows), bf16),
                pltpu.VMEM((columns, rows), bf16),
            ]
            + last_scratch,
            cost_estimate=attention_cost(rows, rows, HEADS),
            compiler_params=params(),
            name="far_finish",
        )(
            dest, packed, near, from_next, from_prior, from_across, query, keys, values, norms,
            gain_first, w_query_key, w_value, w_out, gain_second, w_up, w_down,
        )
    else:
        targets = dest // clusters
        members = lax.rem(targets - lax.axis_index("ball") + lanes, lanes)
        present = jnp.zeros((lanes,), jnp.int32).at[members].set(1)
        slot = jnp.cumsum(present) - present
        blocks = packed.reshape(owners, share, columns)
        empty = jnp.zeros((owners, share, columns), bf16)
        arrived, back = empty, empty

        def picked(source, offset):
            return lax.dynamic_index_in_dim(source, jnp.minimum(slot[offset], owners - 1), 0, False)

        def put(target, offset, block):
            index = jnp.minimum(slot[offset], owners - 1)
            placed = lax.dynamic_update_index_in_dim(target, block, index, 0)
            return jnp.where(present[offset] == 1, placed, target)

        for offset in range(lanes):
            block = picked(blocks, offset)
            arrived = put(arrived, offset, shift(block, offset) if offset else block)
        far_rotated = pl.pallas_call(
            functools.partial(owner_far_kernel, head_size),
            out_shape=wide,
            in_specs=[in_vmem()] * 4,
            out_specs=in_vmem(),
            scratch_shapes=[
                pltpu.VMEM((columns, rows), bf16),
                pltpu.VMEM((rows, columns), bf16),
                pltpu.VMEM((HEADS, tall, rows), bf16),
                pltpu.VMEM((columns, rows), bf16),
            ],
            cost_estimate=attention_cost(rows, rows, HEADS),
            compiler_params=params(),
            name="owner_far",
        )(arrived.reshape(rows, columns), gain_first, w_query_key, w_value)
        leaving = far_rotated.reshape(owners, share, columns)
        for offset in range(lanes):
            block = picked(leaving, offset)
            back = put(back, offset, shift(block, lanes - offset) if offset else block)
        block_out = pl.pallas_call(
            functools.partial(finish_kernel, lanes, clusters),
            out_shape=wide,
            in_specs=[in_smem()] + [in_vmem()] * 7,
            out_specs=anywhere(),
            scratch_shapes=last_scratch,
            cost_estimate=cost(20 * rows * columns * columns, 8 * rows * columns),
            compiler_params=params(),
            name="finish",
        )(
            dest, packed, near, back.reshape(rows, columns).T, w_out, gain_second, w_up, w_down
        )
    return block_out.reshape(points.shape)


def solution(mesh):
    placed = (
        P("ball", "region", None, None),
        P(),
        P(),
        P(),
        P(),
        P(),
        P(),
        P(),
        P("ball", "region", None),
    )
    return jax.shard_map(
        per_device,
        mesh=mesh,
        in_specs=placed,
        out_specs=P("ball", "region", None, None),
        check_vma=False,
    )
```

```python
import functools
import math

import jax
import jax.numpy as jnp
from jax import lax
from jax.experimental import pallas as pl
from jax.experimental.pallas import tpu as pltpu
from jax.sharding import PartitionSpec as P

HEADS = 8
CLUSTER = 64
POOL = 16
TILE = 128
SLOW_BLOCK = 256
QUERY_BLOCK = 512
KEY_BLOCK = 256
AHEAD = 3
ROW_BLOCK = 256
SAFE_EXPONENT = 104.0
VMEM_LIMIT = 48 * 1024 * 1024

bf16 = jnp.bfloat16
f32 = jnp.float32


def in_vmem():
    return pl.BlockSpec(memory_space=pltpu.VMEM)


def in_smem():
    return pl.BlockSpec(memory_space=pltpu.SMEM)


def in_hbm():
    return pl.BlockSpec(memory_space=pltpu.HBM)


def anywhere():
    return pl.BlockSpec(memory_space=pl.ANY)


def params():
    return pltpu.CompilerParams(vmem_limit_bytes=VMEM_LIMIT)


def cost(flops, moved, transcendentals=0):
    return pl.CostEstimate(
        flops=int(flops), bytes_accessed=int(moved), transcendentals=int(transcendentals)
    )


def rms_norm(rows, gain):
    widened = rows.astype(f32)
    scaling = lax.rsqrt(jnp.mean(widened * widened, axis=1, keepdims=True) + 1e-06)
    return (widened * scaling * gain).astype(bf16)


def dot32(left, right):
    return jnp.dot(left, right, preferred_element_type=f32)


def packed_places(dest_ref, clusters, lanes, slots, counts):
    me = lax.axis_index("ball")
    capacity = 2 * clusters // lanes
    offsets = []
    for offset in range(lanes):
        slots[offset] = 0
        counts[offset] = 0
    for cluster in range(clusters):
        offset = lax.rem(dest_ref[cluster] // clusters - me + lanes, lanes)
        slots[offset] = 1
        offsets.append(offset)
    if capacity * 2 == clusters:
        low, high = offsets[0], offsets[0]
        for offset in offsets[1:]:
            low, high = jnp.minimum(low, offset), jnp.maximum(high, offset)
        swap = high - low > lanes // 2
        slots[low] = jnp.where(swap, 1, 0)
        slots[high] = jnp.where(swap, 0, 1)
        across = high - low == lanes // 2
    else:
        taken = 0
        for offset in range(lanes):
            here = slots[offset]
            slots[offset] = taken
            taken = taken + here
        across = None
    places = []
    for offset in offsets:
        rank = counts[offset]
        counts[offset] = rank + 1
        place = (slots[offset] * capacity + rank) * CLUSTER
        places.append(pl.multiple_of(place, CLUSTER))
    return places, across


def factor_of(head_size):
    return math.log2(math.e) / math.sqrt(head_size)


def extended_values(values, head_size):
    columns, rows = values.shape[1], values.shape[0]
    turned = values.T
    ones = jnp.ones((16, rows), bf16)
    return [
        jnp.concatenate([turned[h * head_size : (h + 1) * head_size], ones], axis=0)
        for h in range(columns // head_size)
    ]


def masked_query(query, head, head_size):
    row = lax.broadcasted_iota(jnp.int32, (TILE, 1), 0) // head_size
    return jnp.where(row == head % (TILE // head_size), query, bf16(0))


def run_jobs(jobs, ahead=AHEAD):
    waiting = [first() for first, _ in jobs[:ahead]]
    for index, (_, second) in enumerate(jobs):
        if index + ahead < len(jobs):
            waiting.append(jobs[index + ahead][0]())
        second(waiting.pop(0))


def plain_weights(scores, head_size):
    return jnp.exp2(scores * factor_of(head_size)).astype(bf16)


def attention_jobs(qt_ref, columns_of_query, heads, parts_of, head_size, store):
    per_tile = TILE // head_size
    kept = head_size + 8
    sums = {}
    jobs = []

    def job(start, head, key_ref, value_ref, first, last):
        tile = slice(head // per_tile * TILE, (head // per_tile + 1) * TILE)
        queries = slice(start, start + QUERY_BLOCK)
        rows = slice(first, first + KEY_BLOCK)

        def scores():
            query = masked_query(qt_ref[tile, queries], head, head_size)
            return dot32(key_ref[rows, tile], query)

        def mix(values):
            mixed = dot32(value_ref[head, :, rows], plain_weights(values, head_size))[:kept]
            if (start, head) in sums:
                mixed = mixed + sums.pop((start, head))
            if last:
                store(head, queries, mixed)
            else:
                sums[start, head] = mixed

        return scores, mix

    for start in columns_of_query:
        for head in heads:
            blocks = [
                (keys, values, row)
                for keys, values, first, end in parts_of(start)
                for row in range(first, end, KEY_BLOCK)
            ]
            for index, (keys, values, row) in enumerate(blocks):
                jobs.append(job(start, head, keys, values, row, index + 1 == len(blocks)))
    return jobs


def divided(sums, head_size):
    return (sums[:head_size] / sums[head_size : head_size + 1]).astype(bf16)


def head_norms(rows, head_size):
    columns = rows.shape[1]
    widened = rows.astype(f32)
    channel = lax.broadcasted_iota(jnp.int32, (columns, TILE), 0) // head_size
    head = lax.broadcasted_iota(jnp.int32, (columns, TILE), 1)
    members = (channel == head).astype(bf16)
    return jnp.max(dot32((widened * widened).astype(bf16), members), axis=0, keepdims=True)


def exponents_safe(query_norms, key_norms, head_size):
    limit = (SAFE_EXPONENT / factor_of(head_size)) ** 2
    return jnp.max(query_norms * key_norms) <= limit


def shifted_attention(qt_ref, start, count, parts, head_size, out_ref):
    per_tile = TILE // head_size

    def step(index, carry):
        head = index % HEADS
        block = pl.multiple_of(start + index // HEADS * SLOW_BLOCK, SLOW_BLOCK)
        tile = pl.multiple_of(head // per_tile * TILE, TILE)
        query = masked_query(
            qt_ref[pl.ds(tile, TILE), pl.ds(block, SLOW_BLOCK)], head, head_size
        )
        loaded = [part(pl.ds(tile, TILE), head) for part in parts]
        scores = [dot32(keys, query) for keys, _ in loaded]
        top = jnp.max(scores[0], axis=0, keepdims=True)
        for more in scores[1:]:
            top = jnp.maximum(top, jnp.max(more, axis=0, keepdims=True))
        mixed = 0.0
        for block_scores, (_, values) in zip(scores, loaded):
            mixed = mixed + dot32(values, plain_weights(block_scores - top, head_size))
        rows = pl.ds(pl.multiple_of(head * head_size, head_size), head_size)
        out_ref[rows, pl.ds(block, SLOW_BLOCK)] = (
            mixed[:head_size] / mixed[head_size : head_size + 1]
        ).astype(bf16)
        return carry

    lax.fori_loop(0, HEADS * (count // SLOW_BLOCK), step, 0)


def gelu(value):
    slope = math.sqrt(2.0 / math.pi)
    inner = value * (value * value * (0.044715 * slope) + slope)
    half = 0.5 * value
    return half + half * jnp.tanh(inner)


def pack_kernel(
    lanes, clusters, dest_hbm, points_ref, gain_first, gain_second, packed_ref, first_ref,
    second_ref, dest_ref, dest, slots, counts, sems,
):
    fetch = pltpu.make_async_copy(dest_hbm, dest, sems.at[clusters])
    fetch.start()
    moved = [
        pltpu.make_async_copy(gain_first, first_ref, sems.at[clusters + 1]),
        pltpu.make_async_copy(gain_second, second_ref, sems.at[clusters + 2]),
        pltpu.make_async_copy(dest_hbm, dest_ref, sems.at[clusters + 3]),
    ]
    for copy in moved:
        copy.start()
    fetch.wait()
    places, _ = packed_places(dest, clusters, lanes, slots, counts)
    copies = [
        pltpu.make_async_copy(
            points_ref.at[pl.ds(cluster * CLUSTER, CLUSTER)],
            packed_ref.at[pl.ds(place, CLUSTER)],
            sems.at[cluster],
        )
        for cluster, place in enumerate(places)
    ]
    for copy in copies:
        copy.start()
    for copy in moved + copies:
        copy.wait()


def project_kernel(
    head_size, packed_ref, gain_ref, wqk_ref, wv_ref, qt_ref, k_ref, vt_ref, pool_ref, facts_ref
):
    rows, columns = packed_ref.shape
    normed = rms_norm(packed_ref[...], gain_ref[...])
    paired = dot32(normed, wqk_ref[...]).astype(bf16)
    values = dot32(normed, wv_ref[...]).astype(bf16)
    query, keys = paired[:, :columns], paired[:, columns:]
    k_ref[...] = keys
    pooled = rows // POOL
    row = lax.broadcasted_iota(jnp.int32, (pooled, rows), 0)
    column = lax.broadcasted_iota(jnp.int32, (pooled, rows), 1)
    averaging = jnp.where(column // POOL == row, 1.0 / math.sqrt(POOL), 0.0).astype(bf16)
    pool_ref[:pooled] = dot32(averaging, keys).astype(bf16)
    pool_ref[pooled:] = dot32(averaging, values).astype(bf16)
    qt_ref[...] = query.T
    for head, extended in enumerate(extended_values(values, head_size)):
        vt_ref[head] = extended
    facts_ref[0:1] = head_norms(query, head_size)
    facts_ref[1:2] = head_norms(keys, head_size)


def near_part_kernel(heads, head_size, qt_ref, k_ref, vt_ref, o_ref):
    rows = k_ref.shape[0]

    def store(head, queries, sums):
        o_ref[head - heads[0], :, queries] = sums

    run_jobs(
        attention_jobs(
            qt_ref,
            range(0, rows, QUERY_BLOCK),
            heads,
            lambda start: [(k_ref, vt_ref, 0, rows)],
            head_size,
            store,
        )
    )


def near_kernel(head_size, qt_ref, k_ref, vt_ref, facts_ref, pool_ref, *rest):
    partial = [(ref, inner) for ref in rest[:-3] for inner in range(ref.shape[0])]
    y_ref, kp_ref, vp_ref = rest[-3:]
    rows = k_ref.shape[0]
    regions, pooled = pool_ref.shape[0], pool_ref.shape[1] // 2
    for region in range(regions):
        kp_ref[region * pooled : (region + 1) * pooled] = pool_ref[region, :pooled]
    gathered = jnp.concatenate([pool_ref[r, pooled:] for r in range(regions)], axis=0)
    for head, extended in enumerate(extended_values(gathered, head_size)):
        vp_ref[head] = extended
    key_norms = jnp.maximum(facts_ref[1:2], head_norms(kp_ref[...], head_size))
    safe = exponents_safe(facts_ref[0:1], key_norms, head_size)

    def store(head, queries, sums):
        ref, inner = partial[head]
        sums = sums + ref[inner, :, queries]
        y_ref[head * head_size : (head + 1) * head_size, queries] = divided(sums, head_size)

    run_jobs(
        attention_jobs(
            qt_ref,
            range(0, rows, QUERY_BLOCK),
            range(HEADS),
            lambda start: [(kp_ref, vp_ref, 0, regions * pooled)],
            head_size,
            store,
        )
    )

    @pl.when(jnp.logical_not(safe))
    def _():
        shifted_attention(
            qt_ref,
            0,
            rows,
            [
                lambda tile, head: (k_ref[:, tile], vt_ref[head]),
                lambda tile, head: (kp_ref[:, tile], vp_ref[head]),
            ],
            head_size,
            y_ref,
        )


class OutputRows:
    def __init__(
        self, places, points_ref, near_ref, far_ref, wo_ref, gain_ref, up_ref, down_ref, out_ref,
        done_ref, origin, sems,
    ):
        for cluster, place in enumerate(places):
            origin[place // CLUSTER] = cluster
        self.refs = points_ref, near_ref, far_ref, wo_ref, gain_ref, up_ref, down_ref
        self.out_ref, self.done_ref, self.origin, self.sems = out_ref, done_ref, origin, sems
        self.rows = points_ref.shape[0]

    def back(self, slot):
        target = pl.multiple_of(self.origin[slot] * CLUSTER, CLUSTER)
        return pltpu.make_async_copy(
            self.done_ref.at[pl.ds(slot * CLUSTER, CLUSTER)],
            self.out_ref.at[pl.ds(target, CLUSTER)],
            self.sems.at[slot],
        )

    def job(self, start):
        points_ref, near_ref, far_ref, wo_ref, gain_ref, up_ref, down_ref = self.refs
        block = slice(start, start + ROW_BLOCK)

        def widen():
            after = (
                points_ref[block].astype(f32)
                + dot32(near_ref[:, block].T, wo_ref[...])
                + dot32(far_ref[:, block].T, wo_ref[...])
            ).astype(bf16)
            return after, dot32(rms_norm(after, gain_ref[...]), up_ref[...])

        def narrow(widened):
            after, hidden = widened
            hidden = gelu(hidden).astype(bf16)
            self.done_ref[block] = (after.astype(f32) + dot32(hidden, down_ref[...])).astype(bf16)
            for slot in range(start // CLUSTER, (start + ROW_BLOCK) // CLUSTER):
                self.back(slot).start()

        return widen, narrow

    def jobs(self, first, end):
        return [self.job(start) for start in range(first, end, ROW_BLOCK)]

    def wait(self):
        for slot in range(self.rows // CLUSTER):
            self.back(slot).wait()


def far_finish_kernel(
    lanes, clusters, head_size, dest_ref, points_ref, near_ref, next_ref, prior_ref, across_ref,
    qt_ref, k_ref, vt_ref, facts_ref, gain_ref, gain_second, wqk_ref, wv_ref, wo_ref, up_ref,
    down_ref, out_ref, kr_ref, vr_ref, y_ref, done_ref, slots, counts, origin, sems,
):
    places, across = packed_places(dest_ref, clusters, lanes, slots, counts)
    output = OutputRows(
        places, points_ref, near_ref, y_ref, wo_ref, gain_second, up_ref, down_ref, out_ref,
        done_ref, origin, sems,
    )
    rows, columns = k_ref.shape
    half = rows // 2
    apart = jnp.concatenate([next_ref[...], prior_ref[...]], axis=0)
    normed = rms_norm(jnp.where(across, across_ref[...], apart), gain_ref[...])
    keys = dot32(normed, wqk_ref[:, columns:]).astype(bf16)
    values = dot32(normed, wv_ref[...]).astype(bf16)
    kr_ref[...] = keys
    for head, extended in enumerate(extended_values(values, head_size)):
        vr_ref[head] = extended
    key_norms = jnp.maximum(facts_ref[1:2], head_norms(keys, head_size))
    safe = exponents_safe(facts_ref[0:1], key_norms, head_size)

    def store(head, queries, sums):
        y_ref[head * head_size : (head + 1) * head_size, queries] = divided(sums, head_size)

    def parts_of(start):
        mine = start // half * half
        other = half - mine
        return [(k_ref, vt_ref, mine, mine + half), (kr_ref, vr_ref, other, other + half)]

    def attend(start, end):
        return attention_jobs(
            qt_ref, range(start, end, QUERY_BLOCK), range(HEADS), parts_of, head_size, store
        )

    run_jobs(attend(0, rows))
    run_jobs(output.jobs(0, rows), ahead=1)
    output.wait()

    @pl.when(jnp.logical_not(safe))
    def _():
        for start in (0, half):
            mine, other = slice(start, start + half), slice(half - start, rows - start)
            shifted_attention(
                qt_ref,
                start,
                half,
                [
                    lambda tile, head, mine=mine: (k_ref[mine, tile], vt_ref[head, :, mine]),
                    lambda tile, head, other=other: (kr_ref[other, tile], vr_ref[head, :, other]),
                ],
                head_size,
                y_ref,
            )
        run_jobs(output.jobs(0, rows), ahead=1)
        output.wait()


def finish_kernel(
    lanes, clusters, dest_ref, points_ref, near_ref, far_ref, wo_ref, gain_ref, up_ref, down_ref,
    out_ref, done_ref, slots, counts, origin, sems,
):
    places, _ = packed_places(dest_ref, clusters, lanes, slots, counts)
    output = OutputRows(
        places, points_ref, near_ref, far_ref, wo_ref, gain_ref, up_ref, down_ref, out_ref,
        done_ref, origin, sems,
    )
    run_jobs(output.jobs(0, output.rows), ahead=1)
    output.wait()


def owner_far_kernel(head_size, x_ref, gain_ref, wqk_ref, wv_ref, out_ref, qt, k, vt, y):
    rows, columns = x_ref.shape
    normed = rms_norm(x_ref[...], gain_ref[...])
    paired = dot32(normed, wqk_ref[...]).astype(bf16)
    values = dot32(normed, wv_ref[...]).astype(bf16)
    qt[...] = paired[:, :columns].T
    k[...] = paired[:, columns:]
    for head, extended in enumerate(extended_values(values, head_size)):
        vt[head] = extended
    shifted_attention(
        qt, 0, rows, [lambda tile, head: (k[:, tile], vt[head])], head_size, y
    )
    out_ref[...] = y[...].T


def per_device(
    points, gain_attn, w_query_key, w_value, w_out, gain_mlp, w_up, w_down, cluster_dest
):
    columns = points.shape[-1]
    flat = points.reshape(-1, columns)
    rows = flat.shape[0]
    lanes, regions = lax.axis_size("ball"), lax.axis_size("region")
    clusters = rows // CLUSTER
    share = 2 * clusters // lanes * CLUSTER
    owners = rows // share
    pooled = rows // POOL
    head_size = columns // HEADS
    tall = head_size + 16
    kept = head_size + 8
    dest = cluster_dest.reshape(clusters)
    gain_first = gain_attn.reshape(1, columns)
    gain_second = gain_mlp.reshape(1, columns)
    wide = jax.ShapeDtypeStruct((rows, columns), bf16)
    turned = jax.ShapeDtypeStruct((columns, rows), bf16)
    extended = jax.ShapeDtypeStruct((HEADS, tall, rows), bf16)
    scalars = [pltpu.SMEM((lanes,), jnp.int32)] * 2

    def attention_cost(queries, keys, heads):
        return cost(3 * heads * queries * keys * 256, 4 * rows * columns, heads * queries * keys)

    def shift(data, offset):
        return lax.ppermute(data, "ball", [(i, (i + offset) % lanes) for i in range(lanes)])

    row_of_gains = jax.ShapeDtypeStruct((1, columns), f32)
    packed, gain_first, gain_second, dest = pl.pallas_call(
        functools.partial(pack_kernel, lanes, clusters),
        out_shape=[wide, row_of_gains, row_of_gains, jax.ShapeDtypeStruct(dest.shape, jnp.int32)],
        in_specs=[in_hbm()] * 4,
        out_specs=[anywhere()] * 4,
        scratch_shapes=[pltpu.SMEM((clusters,), jnp.int32)]
        + scalars
        + [pltpu.SemaphoreType.DMA((clusters + 4,))],
        cost_estimate=cost(0, 4 * rows * columns),
        compiler_params=params(),
        name="pack",
    )(
        *(
            pltpu.with_memory_space_constraint(held, pltpu.HBM)
            for held in (dest, flat, gain_first, gain_second)
        )
    )

    pair_path = owners == 2 and lanes == 4
    if pair_path:
        from_across = shift(packed, 2)
        from_next = shift(packed[:share], lanes - 1)
        from_prior = shift(packed[share:], 1)

    query, keys, values, pool, facts = pl.pallas_call(
        functools.partial(project_kernel, head_size),
        out_shape=[
            turned,
            wide,
            extended,
            jax.ShapeDtypeStruct((2 * pooled, columns), bf16),
            jax.ShapeDtypeStruct((8, TILE), f32),
        ],
        in_specs=[in_vmem()] * 4,
        out_specs=[in_vmem()] * 5,
        cost_estimate=cost(6 * rows * columns * columns, 10 * rows * columns),
        compiler_params=params(),
        name="project",
    )(packed, gain_first, w_query_key, w_value)

    def across_regions(data, mask):
        return lax.ppermute(data, "region", [(i, i ^ mask) for i in range(regions)])

    gathered = pool.reshape(1, 2 * pooled, columns)
    step = regions // 2
    while step:
        gathered = jnp.concatenate([gathered, across_regions(gathered, step)], axis=0)
        step //= 2
    partial = [
        pl.pallas_call(
            functools.partial(near_part_kernel, heads, head_size),
            out_shape=jax.ShapeDtypeStruct((len(heads), kept, rows), f32),
            in_specs=[in_vmem()] * 3,
            out_specs=in_vmem(),
            cost_estimate=attention_cost(rows, rows, len(heads)),
            compiler_params=params(),
            name="near_part",
        )(query, keys, values)
        for heads in (range(HEADS // 2), range(HEADS // 2, HEADS))
    ]

    near = pl.pallas_call(
        functools.partial(near_kernel, head_size),
        out_shape=turned,
        in_specs=[in_vmem()] * (5 + len(partial)),
        out_specs=in_vmem(),
        scratch_shapes=[
            pltpu.VMEM((regions * pooled, columns), bf16),
            pltpu.VMEM((HEADS, tall, regions * pooled), bf16),
        ],
        cost_estimate=attention_cost(rows, regions * pooled, HEADS),
        compiler_params=params(),
        name="near",
    )(query, keys, values, facts, gathered, *partial)

    last_scratch = (
        [pltpu.VMEM((rows, columns), bf16)]
        + scalars
        + [pltpu.SMEM((clusters,), jnp.int32), pltpu.SemaphoreType.DMA((clusters,))]
    )
    if pair_path:
        block_out = pl.pallas_call(
            functools.partial(far_finish_kernel, lanes, clusters, head_size),
            out_shape=wide,
            in_specs=[in_smem()] + [in_vmem()] * 16,
            out_specs=anywhere(),
            scratch_shapes=[
                pltpu.VMEM((rows, columns), bf16),
                pltpu.VMEM((HEADS, tall, rows), bf16),
                pltpu.VMEM((columns, rows), bf16),
            ]
            + last_scratch,
            cost_estimate=attention_cost(rows, rows, HEADS),
            compiler_params=params(),
            name="far_finish",
        )(
            dest, packed, near, from_next, from_prior, from_across, query, keys, values, facts,
            gain_first, gain_second, w_query_key, w_value, w_out, w_up, w_down,
        )
    else:
        targets = dest // clusters
        members = lax.rem(targets - lax.axis_index("ball") + lanes, lanes)
        present = jnp.zeros((lanes,), jnp.int32).at[members].set(1)
        slot = jnp.cumsum(present) - present
        blocks = packed.reshape(owners, share, columns)
        empty = jnp.zeros((owners, share, columns), bf16)
        arrived, back = empty, empty

        def picked(source, offset):
            return lax.dynamic_index_in_dim(source, jnp.minimum(slot[offset], owners - 1), 0, False)

        def put(target, offset, block):
            index = jnp.minimum(slot[offset], owners - 1)
            placed = lax.dynamic_update_index_in_dim(target, block, index, 0)
            return jnp.where(present[offset] == 1, placed, target)

        for offset in range(lanes):
            block = picked(blocks, offset)
            arrived = put(arrived, offset, shift(block, offset) if offset else block)
        far_rotated = pl.pallas_call(
            functools.partial(owner_far_kernel, head_size),
            out_shape=wide,
            in_specs=[in_vmem()] * 4,
            out_specs=in_vmem(),
            scratch_shapes=[
                pltpu.VMEM((columns, rows), bf16),
                pltpu.VMEM((rows, columns), bf16),
                pltpu.VMEM((HEADS, tall, rows), bf16),
                pltpu.VMEM((columns, rows), bf16),
            ],
            cost_estimate=attention_cost(rows, rows, HEADS),
            compiler_params=params(),
            name="owner_far",
        )(arrived.reshape(rows, columns), gain_first, w_query_key, w_value)
        leaving = far_rotated.reshape(owners, share, columns)
        for offset in range(lanes):
            block = picked(leaving, offset)
            back = put(back, offset, shift(block, lanes - offset) if offset else block)
        block_out = pl.pallas_call(
            functools.partial(finish_kernel, lanes, clusters),
            out_shape=wide,
            in_specs=[in_smem()] + [in_vmem()] * 7,
            out_specs=anywhere(),
            scratch_shapes=last_scratch,
            cost_estimate=cost(20 * rows * columns * columns, 8 * rows * columns),
            compiler_params=params(),
            name="finish",
        )(
            dest, packed, near, back.reshape(rows, columns).T, w_out, gain_second, w_up, w_down
        )
    return block_out.reshape(points.shape)


def solution(mesh):
    placed = (
        P("ball", "region", None, None),
        P(),
        P(),
        P(),
        P(),
        P(),
        P(),
        P(),
        P("ball", "region", None),
    )
    return jax.shard_map(
        per_device,
        mesh=mesh,
        in_specs=placed,
        out_specs=P("ball", "region", None, None),
        check_vma=False,
    )
```

```python
import functools
import math

import jax
import jax.numpy as jnp
from jax import lax
from jax.experimental import pallas as pl
from jax.experimental.pallas import tpu as pltpu
from jax.sharding import PartitionSpec as P

HEADS = 8
CLUSTER = 64
POOL = 16
TILE = 128
SLOW_BLOCK = 256
QUERY_BLOCK = 512
KEY_BLOCK = 256
AHEAD = 2
PREPARE_AFTER = 4
FIRST_HEADS = 5
ROW_BLOCK = 256
SAFE_EXPONENT = 104.0
VMEM_LIMIT = 48 * 1024 * 1024

bf16 = jnp.bfloat16
f32 = jnp.float32


def in_vmem():
    return pl.BlockSpec(memory_space=pltpu.VMEM)


def in_smem():
    return pl.BlockSpec(memory_space=pltpu.SMEM)


def in_hbm():
    return pl.BlockSpec(memory_space=pltpu.HBM)


def anywhere():
    return pl.BlockSpec(memory_space=pl.ANY)


def params():
    return pltpu.CompilerParams(vmem_limit_bytes=VMEM_LIMIT)


def cost(flops, moved, transcendentals=0):
    return pl.CostEstimate(
        flops=int(flops), bytes_accessed=int(moved), transcendentals=int(transcendentals)
    )


def rms_norm(rows, gain):
    widened = rows.astype(f32)
    scaling = lax.rsqrt(jnp.mean(widened * widened, axis=1, keepdims=True) + 1e-06)
    return (widened * scaling * gain).astype(bf16)


def dot32(left, right):
    return jnp.dot(left, right, preferred_element_type=f32)


def packed_places(dest_ref, clusters, lanes, slots, counts):
    me = lax.axis_index("ball")
    capacity = 2 * clusters // lanes
    offsets = []
    for offset in range(lanes):
        slots[offset] = 0
        counts[offset] = 0
    for cluster in range(clusters):
        offset = lax.rem(dest_ref[cluster] // clusters - me + lanes, lanes)
        slots[offset] = 1
        offsets.append(offset)
    if capacity * 2 == clusters:
        low, high = offsets[0], offsets[0]
        for offset in offsets[1:]:
            low, high = jnp.minimum(low, offset), jnp.maximum(high, offset)
        swap = high - low > lanes // 2
        slots[low] = jnp.where(swap, 1, 0)
        slots[high] = jnp.where(swap, 0, 1)
        across = high - low == lanes // 2
    else:
        taken = 0
        for offset in range(lanes):
            here = slots[offset]
            slots[offset] = taken
            taken = taken + here
        across = None
    places = []
    for offset in offsets:
        rank = counts[offset]
        counts[offset] = rank + 1
        place = (slots[offset] * capacity + rank) * CLUSTER
        places.append(pl.multiple_of(place, CLUSTER))
    return places, across


def factor_of(head_size):
    return math.log2(math.e) / math.sqrt(head_size)


def extended_values(values, head_size):
    columns, rows = values.shape[1], values.shape[0]
    turned = values.T
    ones = jnp.ones((16, rows), bf16)
    return [
        jnp.concatenate([turned[h * head_size : (h + 1) * head_size], ones], axis=0)
        for h in range(columns // head_size)
    ]


def masked_query(query, head, head_size):
    row = lax.broadcasted_iota(jnp.int32, (TILE, 1), 0) // head_size
    return jnp.where(row == head % (TILE // head_size), query, bf16(0))


def run_jobs(jobs, ahead=AHEAD):
    waiting = [first() for first, _ in jobs[:ahead]]
    for index, (_, second) in enumerate(jobs):
        if index + ahead < len(jobs):
            waiting.append(jobs[index + ahead][0]())
        second(waiting.pop(0))


def plain_weights(scores, head_size):
    return jnp.exp2(scores * factor_of(head_size)).astype(bf16)


def attention_jobs(qt_ref, columns_of_query, heads, parts_of, head_size, store):
    per_tile = TILE // head_size
    kept = head_size + 8
    sums = {}
    jobs = []

    def job(start, head, key_ref, value_ref, first, last):
        tile = slice(head // per_tile * TILE, (head // per_tile + 1) * TILE)
        queries = slice(start, start + QUERY_BLOCK)
        rows = slice(first, first + KEY_BLOCK)

        def scores():
            query = masked_query(qt_ref[tile, queries], head, head_size)
            return dot32(key_ref[rows, tile], query)

        def mix(values):
            mixed = dot32(value_ref[head, :, rows], plain_weights(values, head_size))[:kept]
            if (start, head) in sums:
                mixed = mixed + sums.pop((start, head))
            if last:
                store(head, queries, mixed)
            else:
                sums[start, head] = mixed

        return scores, mix

    for start in columns_of_query:
        for head in heads:
            blocks = [
                (keys, values, row)
                for keys, values, first, end in parts_of(start)
                for row in range(first, end, KEY_BLOCK)
            ]
            for index, (keys, values, row) in enumerate(blocks):
                jobs.append(job(start, head, keys, values, row, index + 1 == len(blocks)))
    return jobs


def divided(sums, head_size):
    return (sums[:head_size] / sums[head_size : head_size + 1]).astype(bf16)


def head_norms(rows, head_size):
    columns = rows.shape[1]
    widened = rows.astype(f32)
    channel = lax.broadcasted_iota(jnp.int32, (columns, TILE), 0) // head_size
    head = lax.broadcasted_iota(jnp.int32, (columns, TILE), 1)
    members = (channel == head).astype(bf16)
    return jnp.max(dot32((widened * widened).astype(bf16), members), axis=0, keepdims=True)


def exponents_safe(query_norms, key_norms, head_size):
    limit = (SAFE_EXPONENT / factor_of(head_size)) ** 2
    return jnp.max(query_norms * key_norms) <= limit


def shifted_attention(qt_ref, start, count, parts, head_size, out_ref):
    per_tile = TILE // head_size

    def step(index, carry):
        head = index % HEADS
        block = pl.multiple_of(start + index // HEADS * SLOW_BLOCK, SLOW_BLOCK)
        tile = pl.multiple_of(head // per_tile * TILE, TILE)
        query = masked_query(
            qt_ref[pl.ds(tile, TILE), pl.ds(block, SLOW_BLOCK)], head, head_size
        )
        loaded = [part(pl.ds(tile, TILE), head) for part in parts]
        scores = [dot32(keys, query) for keys, _ in loaded]
        top = jnp.max(scores[0], axis=0, keepdims=True)
        for more in scores[1:]:
            top = jnp.maximum(top, jnp.max(more, axis=0, keepdims=True))
        mixed = 0.0
        for block_scores, (_, values) in zip(scores, loaded):
            mixed = mixed + dot32(values, plain_weights(block_scores - top, head_size))
        rows = pl.ds(pl.multiple_of(head * head_size, head_size), head_size)
        out_ref[rows, pl.ds(block, SLOW_BLOCK)] = (
            mixed[:head_size] / mixed[head_size : head_size + 1]
        ).astype(bf16)
        return carry

    lax.fori_loop(0, HEADS * (count // SLOW_BLOCK), step, 0)


def gelu(value):
    slope = math.sqrt(2.0 / math.pi)
    inner = value * (value * value * (0.044715 * slope) + slope)
    half = 0.5 * value
    return half + half * jnp.tanh(inner)


def pack_kernel(
    lanes, clusters, dest_hbm, points_ref, gain_first, gain_second, packed_ref, first_ref,
    second_ref, dest_ref, dest, slots, counts, sems,
):
    fetch = pltpu.make_async_copy(dest_hbm, dest, sems.at[clusters])
    fetch.start()
    moved = [
        pltpu.make_async_copy(gain_first, first_ref, sems.at[clusters + 1]),
        pltpu.make_async_copy(gain_second, second_ref, sems.at[clusters + 2]),
        pltpu.make_async_copy(dest_hbm, dest_ref, sems.at[clusters + 3]),
    ]
    for copy in moved:
        copy.start()
    fetch.wait()
    places, _ = packed_places(dest, clusters, lanes, slots, counts)
    copies = [
        pltpu.make_async_copy(
            points_ref.at[pl.ds(cluster * CLUSTER, CLUSTER)],
            packed_ref.at[pl.ds(place, CLUSTER)],
            sems.at[cluster],
        )
        for cluster, place in enumerate(places)
    ]
    for copy in copies:
        copy.start()
    for copy in moved + copies:
        copy.wait()


def project_kernel(
    head_size, packed_ref, gain_ref, wqk_ref, wv_ref, qt_ref, k_ref, vt_ref, pool_ref, facts_ref
):
    rows, columns = packed_ref.shape
    normed = rms_norm(packed_ref[...], gain_ref[...])
    paired = dot32(normed, wqk_ref[...]).astype(bf16)
    values = dot32(normed, wv_ref[...]).astype(bf16)
    query, keys = paired[:, :columns], paired[:, columns:]
    k_ref[...] = keys
    pooled = rows // POOL
    row = lax.broadcasted_iota(jnp.int32, (pooled, rows), 0)
    column = lax.broadcasted_iota(jnp.int32, (pooled, rows), 1)
    averaging = jnp.where(column // POOL == row, 1.0 / math.sqrt(POOL), 0.0).astype(bf16)
    pool_ref[:pooled] = dot32(averaging, keys).astype(bf16)
    pool_ref[pooled:] = dot32(averaging, values).astype(bf16)
    qt_ref[...] = query.T
    for head, extended in enumerate(extended_values(values, head_size)):
        vt_ref[head] = extended
    facts_ref[0:1] = head_norms(query, head_size)
    facts_ref[1:2] = head_norms(keys, head_size)


def near_part_kernel(heads, head_size, qt_ref, k_ref, vt_ref, o_ref):
    rows = k_ref.shape[0]

    def store(head, queries, sums):
        o_ref[head - heads[0], :, queries] = sums

    run_jobs(
        attention_jobs(
            qt_ref,
            range(0, rows, QUERY_BLOCK),
            heads,
            lambda start: [(k_ref, vt_ref, 0, rows)],
            head_size,
            store,
        )
    )


def near_kernel(head_size, qt_ref, k_ref, vt_ref, facts_ref, pool_ref, *rest):
    partial = [(ref, inner) for ref in rest[:-3] for inner in range(ref.shape[0])]
    y_ref, kp_ref, vp_ref = rest[-3:]
    rows = k_ref.shape[0]
    regions, pooled = pool_ref.shape[0], pool_ref.shape[1] // 2
    for region in range(regions):
        kp_ref[region * pooled : (region + 1) * pooled] = pool_ref[region, :pooled]
    gathered = jnp.concatenate([pool_ref[r, pooled:] for r in range(regions)], axis=0)
    for head, extended in enumerate(extended_values(gathered, head_size)):
        vp_ref[head] = extended
    key_norms = jnp.maximum(facts_ref[1:2], head_norms(kp_ref[...], head_size))
    safe = exponents_safe(facts_ref[0:1], key_norms, head_size)

    def store(head, queries, sums):
        ref, inner = partial[head]
        sums = sums + ref[inner, :, queries]
        y_ref[head * head_size : (head + 1) * head_size, queries] = divided(sums, head_size)

    run_jobs(
        attention_jobs(
            qt_ref,
            range(0, rows, QUERY_BLOCK),
            range(HEADS),
            lambda start: [(kp_ref, vp_ref, 0, regions * pooled)],
            head_size,
            store,
        )
    )

    @pl.when(jnp.logical_not(safe))
    def _():
        shifted_attention(
            qt_ref,
            0,
            rows,
            [
                lambda tile, head: (k_ref[:, tile], vt_ref[head]),
                lambda tile, head: (kp_ref[:, tile], vp_ref[head]),
            ],
            head_size,
            y_ref,
        )


class OutputRows:
    def __init__(
        self, places, points_ref, near_ref, far_ref, wo_ref, gain_ref, up_ref, down_ref, out_ref,
        done_ref, origin, sems,
    ):
        for cluster, place in enumerate(places):
            origin[place // CLUSTER] = cluster
        self.refs = points_ref, near_ref, far_ref, wo_ref, gain_ref, up_ref, down_ref
        self.out_ref, self.done_ref, self.origin, self.sems = out_ref, done_ref, origin, sems
        self.rows = points_ref.shape[0]

    def back(self, slot):
        target = pl.multiple_of(self.origin[slot] * CLUSTER, CLUSTER)
        return pltpu.make_async_copy(
            self.done_ref.at[pl.ds(slot * CLUSTER, CLUSTER)],
            self.out_ref.at[pl.ds(target, CLUSTER)],
            self.sems.at[slot],
        )

    def job(self, start):
        points_ref, near_ref, far_ref, wo_ref, gain_ref, up_ref, down_ref = self.refs
        block = slice(start, start + ROW_BLOCK)

        def widen():
            after = (
                points_ref[block].astype(f32)
                + dot32(near_ref[:, block].T, wo_ref[...])
                + dot32(far_ref[:, block].T, wo_ref[...])
            ).astype(bf16)
            return after, dot32(rms_norm(after, gain_ref[...]), up_ref[...])

        def narrow(widened):
            after, hidden = widened
            hidden = gelu(hidden).astype(bf16)
            self.done_ref[block] = (after.astype(f32) + dot32(hidden, down_ref[...])).astype(bf16)
            for slot in range(start // CLUSTER, (start + ROW_BLOCK) // CLUSTER):
                self.back(slot).start()

        return widen, narrow

    def jobs(self, first, end):
        return [self.job(start) for start in range(first, end, ROW_BLOCK)]

    def wait(self):
        for slot in range(self.rows // CLUSTER):
            self.back(slot).wait()


def far_finish_kernel(
    lanes, clusters, head_size, dest_ref, points_ref, near_ref, next_ref, prior_ref, across_ref,
    qt_ref, k_ref, vt_ref, facts_ref, gain_ref, gain_second, wqk_ref, wv_ref, wo_ref, up_ref,
    down_ref, out_ref, kr_ref, vr_ref, y_ref, done_ref, slots, counts, origin, sems,
):
    places, across = packed_places(dest_ref, clusters, lanes, slots, counts)
    output = OutputRows(
        places, points_ref, near_ref, y_ref, wo_ref, gain_second, up_ref, down_ref, out_ref,
        done_ref, origin, sems,
    )
    rows, columns = k_ref.shape
    half = rows // 2
    found = {}

    def prepare(_):
        apart = jnp.concatenate([next_ref[...], prior_ref[...]], axis=0)
        normed = rms_norm(jnp.where(across, across_ref[...], apart), gain_ref[...])
        keys = dot32(normed, wqk_ref[:, columns:]).astype(bf16)
        values = dot32(normed, wv_ref[...]).astype(bf16)
        kr_ref[...] = keys
        for head, extended in enumerate(extended_values(values, head_size)):
            vr_ref[head] = extended
        key_norms = jnp.maximum(facts_ref[1:2], head_norms(keys, head_size))
        found["safe"] = exponents_safe(facts_ref[0:1], key_norms, head_size)

    def keep(head, queries, sums):
        found[head, queries.start] = sums

    def store(head, queries, sums):
        sums = sums + found.pop((head, queries.start))
        y_ref[head * head_size : (head + 1) * head_size, queries] = divided(sums, head_size)

    def own_part(start):
        mine = start // half * half
        return [(k_ref, vt_ref, mine, mine + half)]

    def arrived_part(start):
        other = half - start // half * half
        return [(kr_ref, vr_ref, other, other + half)]

    def attend(parts_of, finish):
        return attention_jobs(
            qt_ref, range(0, rows, QUERY_BLOCK), range(HEADS), parts_of, head_size, finish
        )

    jobs = attend(own_part, keep)
    jobs.insert(PREPARE_AFTER, (lambda: None, prepare))
    run_jobs(jobs + attend(arrived_part, store))
    safe = found["safe"]
    run_jobs(output.jobs(0, rows), ahead=1)
    output.wait()

    @pl.when(jnp.logical_not(safe))
    def _():
        for start in (0, half):
            mine, other = slice(start, start + half), slice(half - start, rows - start)
            shifted_attention(
                qt_ref,
                start,
                half,
                [
                    lambda tile, head, mine=mine: (k_ref[mine, tile], vt_ref[head, :, mine]),
                    lambda tile, head, other=other: (kr_ref[other, tile], vr_ref[head, :, other]),
                ],
                head_size,
                y_ref,
            )
        run_jobs(output.jobs(0, rows), ahead=1)
        output.wait()


def finish_kernel(
    lanes, clusters, dest_ref, points_ref, near_ref, far_ref, wo_ref, gain_ref, up_ref, down_ref,
    out_ref, done_ref, slots, counts, origin, sems,
):
    places, _ = packed_places(dest_ref, clusters, lanes, slots, counts)
    output = OutputRows(
        places, points_ref, near_ref, far_ref, wo_ref, gain_ref, up_ref, down_ref, out_ref,
        done_ref, origin, sems,
    )
    run_jobs(output.jobs(0, output.rows), ahead=1)
    output.wait()


def owner_far_kernel(head_size, x_ref, gain_ref, wqk_ref, wv_ref, out_ref, qt, k, vt, y):
    rows, columns = x_ref.shape
    normed = rms_norm(x_ref[...], gain_ref[...])
    paired = dot32(normed, wqk_ref[...]).astype(bf16)
    values = dot32(normed, wv_ref[...]).astype(bf16)
    qt[...] = paired[:, :columns].T
    k[...] = paired[:, columns:]
    for head, extended in enumerate(extended_values(values, head_size)):
        vt[head] = extended
    shifted_attention(
        qt, 0, rows, [lambda tile, head: (k[:, tile], vt[head])], head_size, y
    )
    out_ref[...] = y[...].T


def per_device(
    points, gain_attn, w_query_key, w_value, w_out, gain_mlp, w_up, w_down, cluster_dest
):
    columns = points.shape[-1]
    flat = points.reshape(-1, columns)
    rows = flat.shape[0]
    lanes, regions = lax.axis_size("ball"), lax.axis_size("region")
    clusters = rows // CLUSTER
    share = 2 * clusters // lanes * CLUSTER
    owners = rows // share
    pooled = rows // POOL
    head_size = columns // HEADS
    tall = head_size + 16
    kept = head_size + 8
    dest = cluster_dest.reshape(clusters)
    gain_first = gain_attn.reshape(1, columns)
    gain_second = gain_mlp.reshape(1, columns)
    wide = jax.ShapeDtypeStruct((rows, columns), bf16)
    turned = jax.ShapeDtypeStruct((columns, rows), bf16)
    extended = jax.ShapeDtypeStruct((HEADS, tall, rows), bf16)
    scalars = [pltpu.SMEM((lanes,), jnp.int32)] * 2

    def attention_cost(queries, keys, heads):
        return cost(3 * heads * queries * keys * 256, 4 * rows * columns, heads * queries * keys)

    def shift(data, offset):
        return lax.ppermute(data, "ball", [(i, (i + offset) % lanes) for i in range(lanes)])

    row_of_gains = jax.ShapeDtypeStruct((1, columns), f32)
    packed, gain_first, gain_second, dest = pl.pallas_call(
        functools.partial(pack_kernel, lanes, clusters),
        out_shape=[wide, row_of_gains, row_of_gains, jax.ShapeDtypeStruct(dest.shape, jnp.int32)],
        in_specs=[in_hbm()] * 4,
        out_specs=[anywhere()] * 4,
        scratch_shapes=[pltpu.SMEM((clusters,), jnp.int32)]
        + scalars
        + [pltpu.SemaphoreType.DMA((clusters + 4,))],
        cost_estimate=cost(0, 4 * rows * columns),
        compiler_params=params(),
        name="pack",
    )(
        *(
            pltpu.with_memory_space_constraint(held, pltpu.HBM)
            for held in (dest, flat, gain_first, gain_second)
        )
    )

    pair_path = owners == 2 and lanes == 4
    if pair_path:
        from_across = shift(packed, 2)
        from_next = shift(packed[:share], lanes - 1)
        from_prior = shift(packed[share:], 1)

    query, keys, values, pool, facts = pl.pallas_call(
        functools.partial(project_kernel, head_size),
        out_shape=[
            turned,
            wide,
            extended,
            jax.ShapeDtypeStruct((2 * pooled, columns), bf16),
            jax.ShapeDtypeStruct((8, TILE), f32),
        ],
        in_specs=[in_vmem()] * 4,
        out_specs=[in_vmem()] * 5,
        cost_estimate=cost(6 * rows * columns * columns, 10 * rows * columns),
        compiler_params=params(),
        name="project",
    )(packed, gain_first, w_query_key, w_value)

    def across_regions(data, mask):
        return lax.ppermute(data, "region", [(i, i ^ mask) for i in range(regions)])

    gathered = pool.reshape(1, 2 * pooled, columns)
    step = regions // 2
    while step:
        gathered = jnp.concatenate([gathered, across_regions(gathered, step)], axis=0)
        step //= 2
    partial = [
        pl.pallas_call(
            functools.partial(near_part_kernel, heads, head_size),
            out_shape=jax.ShapeDtypeStruct((len(heads), kept, rows), f32),
            in_specs=[in_vmem()] * 3,
            out_specs=in_vmem(),
            cost_estimate=attention_cost(rows, rows, len(heads)),
            compiler_params=params(),
            name="near_part",
        )(query, keys, values)
        for heads in (range(FIRST_HEADS), range(FIRST_HEADS, HEADS))
    ]

    near = pl.pallas_call(
        functools.partial(near_kernel, head_size),
        out_shape=turned,
        in_specs=[in_vmem()] * (5 + len(partial)),
        out_specs=in_vmem(),
        scratch_shapes=[
            pltpu.VMEM((regions * pooled, columns), bf16),
            pltpu.VMEM((HEADS, tall, regions * pooled), bf16),
        ],
        cost_estimate=attention_cost(rows, regions * pooled, HEADS),
        compiler_params=params(),
        name="near",
    )(query, keys, values, facts, gathered, *partial)

    last_scratch = (
        [pltpu.VMEM((rows, columns), bf16)]
        + scalars
        + [pltpu.SMEM((clusters,), jnp.int32), pltpu.SemaphoreType.DMA((clusters,))]
    )
    if pair_path:
        block_out = pl.pallas_call(
            functools.partial(far_finish_kernel, lanes, clusters, head_size),
            out_shape=wide,
            in_specs=[in_smem()] + [in_vmem()] * 16,
            out_specs=anywhere(),
            scratch_shapes=[
                pltpu.VMEM((rows, columns), bf16),
                pltpu.VMEM((HEADS, tall, rows), bf16),
                pltpu.VMEM((columns, rows), bf16),
            ]
            + last_scratch,
            cost_estimate=attention_cost(rows, rows, HEADS),
            compiler_params=params(),
            name="far_finish",
        )(
            dest, packed, near, from_next, from_prior, from_across, query, keys, values, facts,
            gain_first, gain_second, w_query_key, w_value, w_out, w_up, w_down,
        )
    else:
        targets = dest // clusters
        members = lax.rem(targets - lax.axis_index("ball") + lanes, lanes)
        present = jnp.zeros((lanes,), jnp.int32).at[members].set(1)
        slot = jnp.cumsum(present) - present
        blocks = packed.reshape(owners, share, columns)
        empty = jnp.zeros((owners, share, columns), bf16)
        arrived, back = empty, empty

        def picked(source, offset):
            return lax.dynamic_index_in_dim(source, jnp.minimum(slot[offset], owners - 1), 0, False)

        def put(target, offset, block):
            index = jnp.minimum(slot[offset], owners - 1)
            placed = lax.dynamic_update_index_in_dim(target, block, index, 0)
            return jnp.where(present[offset] == 1, placed, target)

        for offset in range(lanes):
            block = picked(blocks, offset)
            arrived = put(arrived, offset, shift(block, offset) if offset else block)
        far_rotated = pl.pallas_call(
            functools.partial(owner_far_kernel, head_size),
            out_shape=wide,
            in_specs=[in_vmem()] * 4,
            out_specs=in_vmem(),
            scratch_shapes=[
                pltpu.VMEM((columns, rows), bf16),
                pltpu.VMEM((rows, columns), bf16),
                pltpu.VMEM((HEADS, tall, rows), bf16),
                pltpu.VMEM((columns, rows), bf16),
            ],
            cost_estimate=attention_cost(rows, rows, HEADS),
            compiler_params=params(),
            name="owner_far",
        )(arrived.reshape(rows, columns), gain_first, w_query_key, w_value)
        leaving = far_rotated.reshape(owners, share, columns)
        for offset in range(lanes):
            block = picked(leaving, offset)
            back = put(back, offset, shift(block, lanes - offset) if offset else block)
        block_out = pl.pallas_call(
            functools.partial(finish_kernel, lanes, clusters),
            out_shape=wide,
            in_specs=[in_smem()] + [in_vmem()] * 7,
            out_specs=anywhere(),
            scratch_shapes=last_scratch,
            cost_estimate=cost(20 * rows * columns * columns, 8 * rows * columns),
            compiler_params=params(),
            name="finish",
        )(
            dest, packed, near, back.reshape(rows, columns).T, w_out, gain_second, w_up, w_down
        )
    return block_out.reshape(points.shape)


def solution(mesh):
    placed = (
        P("ball", "region", None, None),
        P(),
        P(),
        P(),
        P(),
        P(),
        P(),
        P(),
        P("ball", "region", None),
    )
    return jax.shard_map(
        per_device,
        mesh=mesh,
        in_specs=placed,
        out_specs=P("ball", "region", None, None),
        check_vma=False,
    )
```

```python
import functools
import math

import jax
import jax.numpy as jnp
from jax import lax
from jax.experimental import pallas as pl
from jax.experimental.pallas import tpu as pltpu
from jax.sharding import PartitionSpec as P

HEADS = 8
CLUSTER = 64
POOL = 16
TILE = 128
SLOW_BLOCK = 256
QUERY_BLOCK = 512
KEY_BLOCK = 256
AHEAD = 2
PREPARE_AFTER = 4
FIRST_HEADS = 5
ROW_BLOCK = 256
SAFE_EXPONENT = 104.0
VMEM_LIMIT = 48 * 1024 * 1024

bf16 = jnp.bfloat16
f32 = jnp.float32


def in_vmem():
    return pl.BlockSpec(memory_space=pltpu.VMEM)


def in_smem():
    return pl.BlockSpec(memory_space=pltpu.SMEM)


def in_hbm():
    return pl.BlockSpec(memory_space=pltpu.HBM)


def anywhere():
    return pl.BlockSpec(memory_space=pl.ANY)


def params():
    return pltpu.CompilerParams(vmem_limit_bytes=VMEM_LIMIT)


def cost(flops, moved, transcendentals=0):
    return pl.CostEstimate(
        flops=int(flops), bytes_accessed=int(moved), transcendentals=int(transcendentals)
    )


def rms_norm(rows, gain):
    widened = rows.astype(f32)
    scaling = lax.rsqrt(jnp.mean(widened * widened, axis=1, keepdims=True) + 1e-06)
    return (widened * scaling * gain).astype(bf16)


def dot32(left, right):
    return jnp.dot(left, right, preferred_element_type=f32)


def packed_places(dest_ref, clusters, lanes, slots, counts):
    me = lax.axis_index("ball")
    capacity = 2 * clusters // lanes
    offsets = []
    for offset in range(lanes):
        slots[offset] = 0
        counts[offset] = 0
    for cluster in range(clusters):
        offset = lax.rem(dest_ref[cluster] // clusters - me + lanes, lanes)
        slots[offset] = 1
        offsets.append(offset)
    if capacity * 2 == clusters:
        low, high = offsets[0], offsets[0]
        for offset in offsets[1:]:
            low, high = jnp.minimum(low, offset), jnp.maximum(high, offset)
        swap = high - low > lanes // 2
        slots[low] = jnp.where(swap, 1, 0)
        slots[high] = jnp.where(swap, 0, 1)
        across = high - low == lanes // 2
    else:
        taken = 0
        for offset in range(lanes):
            here = slots[offset]
            slots[offset] = taken
            taken = taken + here
        across = None
    places = []
    for offset in offsets:
        rank = counts[offset]
        counts[offset] = rank + 1
        place = (slots[offset] * capacity + rank) * CLUSTER
        places.append(pl.multiple_of(place, CLUSTER))
    return places, across


def factor_of(head_size):
    return math.log2(math.e) / math.sqrt(head_size)


def extended_values(values, head_size):
    columns, rows = values.shape[1], values.shape[0]
    turned = values.T
    ones = jnp.ones((16, rows), bf16)
    return [
        jnp.concatenate([turned[h * head_size : (h + 1) * head_size], ones], axis=0)
        for h in range(columns // head_size)
    ]


def masked_query(query, head, head_size):
    row = lax.broadcasted_iota(jnp.int32, (TILE, 1), 0) // head_size
    return jnp.where(row == head % (TILE // head_size), query, bf16(0))


def run_jobs(jobs, ahead=AHEAD):
    waiting = [first() for first, _ in jobs[:ahead]]
    for index, (_, second) in enumerate(jobs):
        if index + ahead < len(jobs):
            waiting.append(jobs[index + ahead][0]())
        second(waiting.pop(0))


def plain_weights(scores, head_size):
    return jnp.exp2(scores * factor_of(head_size)).astype(bf16)


def attention_jobs(qt_ref, columns_of_query, heads, parts_of, head_size, store):
    per_tile = TILE // head_size
    kept = head_size + 8
    sums = {}
    jobs = []

    def job(start, head, key_ref, value_ref, first, last):
        tile = slice(head // per_tile * TILE, (head // per_tile + 1) * TILE)
        queries = slice(start, start + QUERY_BLOCK)
        rows = slice(first, first + KEY_BLOCK)

        def scores():
            query = masked_query(qt_ref[tile, queries], head, head_size)
            return dot32(key_ref[rows, tile], query)

        def mix(values):
            mixed = dot32(value_ref[head, :, rows], plain_weights(values, head_size))[:kept]
            if (start, head) in sums:
                mixed = mixed + sums.pop((start, head))
            if last:
                store(head, queries, mixed)
            else:
                sums[start, head] = mixed

        return scores, mix

    for start in columns_of_query:
        for head in heads:
            blocks = [
                (keys, values, row)
                for keys, values, first, end in parts_of(start)
                for row in range(first, end, KEY_BLOCK)
            ]
            for index, (keys, values, row) in enumerate(blocks):
                jobs.append(job(start, head, keys, values, row, index + 1 == len(blocks)))
    return jobs


def divided(sums, head_size):
    return (sums[:head_size] / sums[head_size : head_size + 1]).astype(bf16)


def head_norms(rows, head_size):
    columns = rows.shape[1]
    widened = rows.astype(f32)
    channel = lax.broadcasted_iota(jnp.int32, (columns, TILE), 0) // head_size
    head = lax.broadcasted_iota(jnp.int32, (columns, TILE), 1)
    members = (channel == head).astype(bf16)
    return jnp.max(dot32((widened * widened).astype(bf16), members), axis=0, keepdims=True)


def exponents_safe(query_norms, key_norms, head_size):
    limit = (SAFE_EXPONENT / factor_of(head_size)) ** 2
    return jnp.max(query_norms * key_norms) <= limit


def shifted_attention(qt_ref, start, count, parts, head_size, out_ref):
    per_tile = TILE // head_size

    def step(index, carry):
        head = index % HEADS
        block = pl.multiple_of(start + index // HEADS * SLOW_BLOCK, SLOW_BLOCK)
        tile = pl.multiple_of(head // per_tile * TILE, TILE)
        query = masked_query(
            qt_ref[pl.ds(tile, TILE), pl.ds(block, SLOW_BLOCK)], head, head_size
        )
        loaded = [part(pl.ds(tile, TILE), head) for part in parts]
        scores = [dot32(keys, query) for keys, _ in loaded]
        top = jnp.max(scores[0], axis=0, keepdims=True)
        for more in scores[1:]:
            top = jnp.maximum(top, jnp.max(more, axis=0, keepdims=True))
        mixed = 0.0
        for block_scores, (_, values) in zip(scores, loaded):
            mixed = mixed + dot32(values, plain_weights(block_scores - top, head_size))
        rows = pl.ds(pl.multiple_of(head * head_size, head_size), head_size)
        out_ref[rows, pl.ds(block, SLOW_BLOCK)] = (
            mixed[:head_size] / mixed[head_size : head_size + 1]
        ).astype(bf16)
        return carry

    lax.fori_loop(0, HEADS * (count // SLOW_BLOCK), step, 0)


def gelu(value):
    slope = math.sqrt(2.0 / math.pi)
    inner = value * (value * value * (0.044715 * slope) + slope)
    half = 0.5 * value
    return half + half * jnp.tanh(inner)


def pack_kernel(
    lanes, clusters, dest_hbm, points_ref, gain_first, gain_second, packed_ref, first_ref,
    second_ref, dest_ref, dest, slots, counts, sems,
):
    fetch = pltpu.make_async_copy(dest_hbm, dest, sems.at[clusters])
    fetch.start()
    moved = [
        pltpu.make_async_copy(gain_first, first_ref, sems.at[clusters + 1]),
        pltpu.make_async_copy(gain_second, second_ref, sems.at[clusters + 2]),
        pltpu.make_async_copy(dest_hbm, dest_ref, sems.at[clusters + 3]),
    ]
    for copy in moved:
        copy.start()
    fetch.wait()
    places, _ = packed_places(dest, clusters, lanes, slots, counts)
    copies = [
        pltpu.make_async_copy(
            points_ref.at[pl.ds(cluster * CLUSTER, CLUSTER)],
            packed_ref.at[pl.ds(place, CLUSTER)],
            sems.at[cluster],
        )
        for cluster, place in enumerate(places)
    ]
    for copy in copies:
        copy.start()
    for copy in moved + copies:
        copy.wait()


def project_kernel(
    head_size, packed_ref, gain_ref, wqk_ref, wv_ref, qt_ref, k_ref, vt_ref, pool_ref, facts_ref
):
    rows, columns = packed_ref.shape
    normed = rms_norm(packed_ref[...], gain_ref[...])
    paired = dot32(normed, wqk_ref[...]).astype(bf16)
    values = dot32(normed, wv_ref[...]).astype(bf16)
    query, keys = paired[:, :columns], paired[:, columns:]
    k_ref[...] = keys
    pooled = rows // POOL
    row = lax.broadcasted_iota(jnp.int32, (pooled, rows), 0)
    column = lax.broadcasted_iota(jnp.int32, (pooled, rows), 1)
    averaging = jnp.where(column // POOL == row, 1.0 / math.sqrt(POOL), 0.0).astype(bf16)
    pool_ref[:pooled] = dot32(averaging, keys).astype(bf16)
    pool_ref[pooled:] = dot32(averaging, values).astype(bf16)
    qt_ref[...] = query.T
    for head, extended in enumerate(extended_values(values, head_size)):
        vt_ref[head] = extended
    facts_ref[0:1] = head_norms(query, head_size)
    facts_ref[1:2] = head_norms(keys, head_size)


def near_part_kernel(heads, head_size, qt_ref, k_ref, vt_ref, o_ref):
    rows = k_ref.shape[0]

    def store(head, queries, sums):
        o_ref[head - heads[0], :, queries] = sums

    run_jobs(
        attention_jobs(
            qt_ref,
            range(0, rows, QUERY_BLOCK),
            heads,
            lambda start: [(k_ref, vt_ref, 0, rows)],
            head_size,
            store,
        )
    )


def near_kernel(head_size, qt_ref, k_ref, vt_ref, facts_ref, pool_ref, *rest):
    partial = [(ref, inner) for ref in rest[:-3] for inner in range(ref.shape[0])]
    y_ref, kp_ref, vp_ref = rest[-3:]
    rows = k_ref.shape[0]
    regions, pooled = pool_ref.shape[0], pool_ref.shape[1] // 2
    for region in range(regions):
        kp_ref[region * pooled : (region + 1) * pooled] = pool_ref[region, :pooled]
    gathered = jnp.concatenate([pool_ref[r, pooled:] for r in range(regions)], axis=0)
    for head, extended in enumerate(extended_values(gathered, head_size)):
        vp_ref[head] = extended
    key_norms = jnp.maximum(facts_ref[1:2], head_norms(kp_ref[...], head_size))
    safe = exponents_safe(facts_ref[0:1], key_norms, head_size)

    def store(head, queries, sums):
        ref, inner = partial[head]
        sums = sums + ref[inner, :, queries]
        y_ref[head * head_size : (head + 1) * head_size, queries] = divided(sums, head_size)

    run_jobs(
        attention_jobs(
            qt_ref,
            range(0, rows, QUERY_BLOCK),
            range(HEADS),
            lambda start: [(kp_ref, vp_ref, 0, regions * pooled)],
            head_size,
            store,
        )
    )

    @pl.when(jnp.logical_not(safe))
    def _():
        shifted_attention(
            qt_ref,
            0,
            rows,
            [
                lambda tile, head: (k_ref[:, tile], vt_ref[head]),
                lambda tile, head: (kp_ref[:, tile], vp_ref[head]),
            ],
            head_size,
            y_ref,
        )


class OutputRows:
    def __init__(
        self, places, points_ref, near_ref, far_ref, wo_ref, gain_ref, up_ref, down_ref, out_ref,
        done_ref, origin, sems,
    ):
        for cluster, place in enumerate(places):
            origin[place // CLUSTER] = cluster
        self.refs = points_ref, near_ref, far_ref, wo_ref, gain_ref, up_ref, down_ref
        self.out_ref, self.done_ref, self.origin, self.sems = out_ref, done_ref, origin, sems
        self.rows = points_ref.shape[0]

    def back(self, slot):
        target = pl.multiple_of(self.origin[slot] * CLUSTER, CLUSTER)
        return pltpu.make_async_copy(
            self.done_ref.at[pl.ds(slot * CLUSTER, CLUSTER)],
            self.out_ref.at[pl.ds(target, CLUSTER)],
            self.sems.at[slot],
        )

    def job(self, start):
        points_ref, near_ref, far_ref, wo_ref, gain_ref, up_ref, down_ref = self.refs
        block = slice(start, start + ROW_BLOCK)

        def widen():
            after = (
                points_ref[block].astype(f32)
                + dot32(near_ref[:, block].T, wo_ref[...])
                + dot32(far_ref[:, block].T, wo_ref[...])
            ).astype(bf16)
            return after, dot32(rms_norm(after, gain_ref[...]), up_ref[...])

        def narrow(widened):
            after, hidden = widened
            hidden = gelu(hidden).astype(bf16)
            self.done_ref[block] = (after.astype(f32) + dot32(hidden, down_ref[...])).astype(bf16)
            for slot in range(start // CLUSTER, (start + ROW_BLOCK) // CLUSTER):
                self.back(slot).start()

        return widen, narrow

    def jobs(self, first, end):
        return [self.job(start) for start in range(first, end, ROW_BLOCK)]

    def wait(self):
        for slot in range(self.rows // CLUSTER):
            self.back(slot).wait()


def far_finish_kernel(
    lanes, clusters, head_size, dest_ref, points_ref, near_ref, next_ref, prior_ref, across_ref,
    qt_ref, k_ref, vt_ref, facts_ref, gain_ref, gain_second, wqk_ref, wv_ref, wo_ref, up_ref,
    down_ref, out_ref, kr_ref, vr_ref, y_ref, done_ref, slots, counts, origin, sems,
):
    places, across = packed_places(dest_ref, clusters, lanes, slots, counts)
    output = OutputRows(
        places, points_ref, near_ref, y_ref, wo_ref, gain_second, up_ref, down_ref, out_ref,
        done_ref, origin, sems,
    )
    rows, columns = k_ref.shape
    half = rows // 2
    found = {}

    def prepare(_):
        apart = jnp.concatenate([next_ref[...], prior_ref[...]], axis=0)
        normed = rms_norm(jnp.where(across, across_ref[...], apart), gain_ref[...])
        keys = dot32(normed, wqk_ref[:, columns:]).astype(bf16)
        values = dot32(normed, wv_ref[...]).astype(bf16)
        kr_ref[...] = keys
        for head, extended in enumerate(extended_values(values, head_size)):
            vr_ref[head] = extended
        key_norms = jnp.maximum(facts_ref[1:2], head_norms(keys, head_size))
        found["safe"] = exponents_safe(facts_ref[0:1], key_norms, head_size)

    def keep(head, queries, sums):
        found[head, queries.start] = sums

    def store(head, queries, sums):
        sums = sums + found.pop((head, queries.start))
        y_ref[head * head_size : (head + 1) * head_size, queries] = divided(sums, head_size)

    def own_part(start):
        mine = start // half * half
        return [(k_ref, vt_ref, mine, mine + half)]

    def arrived_part(start):
        other = half - start // half * half
        return [(kr_ref, vr_ref, other, other + half)]

    def attend(parts_of, finish):
        return attention_jobs(
            qt_ref, range(0, rows, QUERY_BLOCK), range(HEADS), parts_of, head_size, finish
        )

    jobs = attend(own_part, keep)
    jobs.insert(PREPARE_AFTER, (lambda: None, prepare))
    run_jobs(jobs + attend(arrived_part, store))
    safe = found["safe"]
    run_jobs(output.jobs(0, rows), ahead=1)
    output.wait()

    @pl.when(jnp.logical_not(safe))
    def _():
        for start in (0, half):
            mine, other = slice(start, start + half), slice(half - start, rows - start)
            shifted_attention(
                qt_ref,
                start,
                half,
                [
                    lambda tile, head, mine=mine: (k_ref[mine, tile], vt_ref[head, :, mine]),
                    lambda tile, head, other=other: (kr_ref[other, tile], vr_ref[head, :, other]),
                ],
                head_size,
                y_ref,
            )
        run_jobs(output.jobs(0, rows), ahead=1)
        output.wait()


def finish_kernel(
    lanes, clusters, dest_ref, points_ref, near_ref, far_ref, wo_ref, gain_ref, up_ref, down_ref,
    out_ref, done_ref, slots, counts, origin, sems,
):
    places, _ = packed_places(dest_ref, clusters, lanes, slots, counts)
    output = OutputRows(
        places, points_ref, near_ref, far_ref, wo_ref, gain_ref, up_ref, down_ref, out_ref,
        done_ref, origin, sems,
    )
    run_jobs(output.jobs(0, output.rows), ahead=1)
    output.wait()


def owner_far_kernel(head_size, x_ref, gain_ref, wqk_ref, wv_ref, out_ref, qt, k, vt, y):
    rows, columns = x_ref.shape
    normed = rms_norm(x_ref[...], gain_ref[...])
    paired = dot32(normed, wqk_ref[...]).astype(bf16)
    values = dot32(normed, wv_ref[...]).astype(bf16)
    qt[...] = paired[:, :columns].T
    k[...] = paired[:, columns:]
    for head, extended in enumerate(extended_values(values, head_size)):
        vt[head] = extended
    shifted_attention(
        qt, 0, rows, [lambda tile, head: (k[:, tile], vt[head])], head_size, y
    )
    out_ref[...] = y[...].T


def per_device(
    points, gain_attn, w_query_key, w_value, w_out, gain_mlp, w_up, w_down, cluster_dest
):
    columns = points.shape[-1]
    flat = points.reshape(-1, columns)
    rows = flat.shape[0]
    lanes, regions = lax.axis_size("ball"), lax.axis_size("region")
    clusters = rows // CLUSTER
    share = 2 * clusters // lanes * CLUSTER
    owners = rows // share
    pooled = rows // POOL
    head_size = columns // HEADS
    tall = head_size + 16
    kept = head_size + 8
    dest = cluster_dest.reshape(clusters)
    gain_first = gain_attn.reshape(1, columns)
    gain_second = gain_mlp.reshape(1, columns)
    wide = jax.ShapeDtypeStruct((rows, columns), bf16)
    turned = jax.ShapeDtypeStruct((columns, rows), bf16)
    extended = jax.ShapeDtypeStruct((HEADS, tall, rows), bf16)
    scalars = [pltpu.SMEM((lanes,), jnp.int32)] * 2

    def attention_cost(queries, keys, heads):
        return cost(3 * heads * queries * keys * 256, 4 * rows * columns, heads * queries * keys)

    def shift(data, offset):
        return lax.ppermute(data, "ball", [(i, (i + offset) % lanes) for i in range(lanes)])

    row_of_gains = jax.ShapeDtypeStruct((1, columns), f32)
    packed, gain_first, gain_second, dest = pl.pallas_call(
        functools.partial(pack_kernel, lanes, clusters),
        out_shape=[wide, row_of_gains, row_of_gains, jax.ShapeDtypeStruct(dest.shape, jnp.int32)],
        in_specs=[in_hbm()] * 4,
        out_specs=[anywhere()] * 4,
        scratch_shapes=[pltpu.SMEM((clusters,), jnp.int32)]
        + scalars
        + [pltpu.SemaphoreType.DMA((clusters + 4,))],
        cost_estimate=cost(0, 4 * rows * columns),
        compiler_params=params(),
        name="pack",
    )(
        *(
            pltpu.with_memory_space_constraint(held, pltpu.HBM)
            for held in (dest, flat, gain_first, gain_second)
        )
    )

    pair_path = owners == 2 and lanes == 4
    if pair_path:
        from_across = shift(packed, 2)
        from_next = shift(packed[:share], lanes - 1)
        from_prior = shift(packed[share:], 1)

    query, keys, values, pool, facts = pl.pallas_call(
        functools.partial(project_kernel, head_size),
        out_shape=[
            turned,
            wide,
            extended,
            jax.ShapeDtypeStruct((2 * pooled, columns), bf16),
            jax.ShapeDtypeStruct((8, TILE), f32),
        ],
        in_specs=[in_vmem()] * 4,
        out_specs=[in_vmem()] * 5,
        cost_estimate=cost(6 * rows * columns * columns, 10 * rows * columns),
        compiler_params=params(),
        name="project",
    )(packed, gain_first, w_query_key, w_value)

    def across_regions(data, mask):
        return lax.ppermute(data, "region", [(i, i ^ mask) for i in range(regions)])

    gathered = pool.reshape(1, 2 * pooled, columns)
    step = regions // 2
    while step:
        gathered = jnp.concatenate([gathered, across_regions(gathered, step)], axis=0)
        step //= 2
    partial = [
        pl.pallas_call(
            functools.partial(near_part_kernel, heads, head_size),
            out_shape=jax.ShapeDtypeStruct((len(heads), kept, rows), f32),
            in_specs=[in_vmem()] * 3,
            out_specs=in_vmem(),
            cost_estimate=attention_cost(rows, rows, HEADS // 2),
            compiler_params=params(),
            name="near_part",
        )(query, keys, values)
        for heads in (range(FIRST_HEADS), range(FIRST_HEADS, HEADS))
    ]

    near = pl.pallas_call(
        functools.partial(near_kernel, head_size),
        out_shape=turned,
        in_specs=[in_vmem()] * (5 + len(partial)),
        out_specs=in_vmem(),
        scratch_shapes=[
            pltpu.VMEM((regions * pooled, columns), bf16),
            pltpu.VMEM((HEADS, tall, regions * pooled), bf16),
        ],
        cost_estimate=attention_cost(rows, regions * pooled, HEADS),
        compiler_params=params(),
        name="near",
    )(query, keys, values, facts, gathered, *partial)

    last_scratch = (
        [pltpu.VMEM((rows, columns), bf16)]
        + scalars
        + [pltpu.SMEM((clusters,), jnp.int32), pltpu.SemaphoreType.DMA((clusters,))]
    )
    if pair_path:
        block_out = pl.pallas_call(
            functools.partial(far_finish_kernel, lanes, clusters, head_size),
            out_shape=wide,
            in_specs=[in_smem()] + [in_vmem()] * 16,
            out_specs=anywhere(),
            scratch_shapes=[
                pltpu.VMEM((rows, columns), bf16),
                pltpu.VMEM((HEADS, tall, rows), bf16),
                pltpu.VMEM((columns, rows), bf16),
            ]
            + last_scratch,
            cost_estimate=attention_cost(rows, rows, HEADS),
            compiler_params=params(),
            name="far_finish",
        )(
            dest, packed, near, from_next, from_prior, from_across, query, keys, values, facts,
            gain_first, gain_second, w_query_key, w_value, w_out, w_up, w_down,
        )
    else:
        targets = dest // clusters
        members = lax.rem(targets - lax.axis_index("ball") + lanes, lanes)
        present = jnp.zeros((lanes,), jnp.int32).at[members].set(1)
        slot = jnp.cumsum(present) - present
        blocks = packed.reshape(owners, share, columns)
        empty = jnp.zeros((owners, share, columns), bf16)
        arrived, back = empty, empty

        def picked(source, offset):
            return lax.dynamic_index_in_dim(source, jnp.minimum(slot[offset], owners - 1), 0, False)

        def put(target, offset, block):
            index = jnp.minimum(slot[offset], owners - 1)
            placed = lax.dynamic_update_index_in_dim(target, block, index, 0)
            return jnp.where(present[offset] == 1, placed, target)

        for offset in range(lanes):
            block = picked(blocks, offset)
            arrived = put(arrived, offset, shift(block, offset) if offset else block)
        far_rotated = pl.pallas_call(
            functools.partial(owner_far_kernel, head_size),
            out_shape=wide,
            in_specs=[in_vmem()] * 4,
            out_specs=in_vmem(),
            scratch_shapes=[
                pltpu.VMEM((columns, rows), bf16),
                pltpu.VMEM((rows, columns), bf16),
                pltpu.VMEM((HEADS, tall, rows), bf16),
                pltpu.VMEM((columns, rows), bf16),
            ],
            cost_estimate=attention_cost(rows, rows, HEADS),
            compiler_params=params(),
            name="owner_far",
        )(arrived.reshape(rows, columns), gain_first, w_query_key, w_value)
        leaving = far_rotated.reshape(owners, share, columns)
        for offset in range(lanes):
            block = picked(leaving, offset)
            back = put(back, offset, shift(block, lanes - offset) if offset else block)
        block_out = pl.pallas_call(
            functools.partial(finish_kernel, lanes, clusters),
            out_shape=wide,
            in_specs=[in_smem()] + [in_vmem()] * 7,
            out_specs=anywhere(),
            scratch_shapes=last_scratch,
            cost_estimate=cost(20 * rows * columns * columns, 8 * rows * columns),
            compiler_params=params(),
            name="finish",
        )(
            dest, packed, near, back.reshape(rows, columns).T, w_out, gain_second, w_up, w_down
        )
    return block_out.reshape(points.shape)


def solution(mesh):
    placed = (
        P("ball", "region", None, None),
        P(),
        P(),
        P(),
        P(),
        P(),
        P(),
        P(),
        P("ball", "region", None),
    )
    return jax.shard_map(
        per_device,
        mesh=mesh,
        in_specs=placed,
        out_specs=P("ball", "region", None, None),
        check_vma=False,
    )
```

```python
import functools
import math

import jax
import jax.numpy as jnp
from jax import lax
from jax.experimental import pallas as pl
from jax.experimental.pallas import tpu as pltpu
from jax.sharding import PartitionSpec as P

HEADS = 8
CLUSTER = 64
POOL = 16
TILE = 128
SLOW_BLOCK = 256
QUERY_BLOCK = 512
KEY_BLOCK = 256
AHEAD = 2
PREPARE_AFTER = 4
FIRST_HEADS = 6
ROW_BLOCK = 256
SAFE_EXPONENT = 104.0
VMEM_LIMIT = 48 * 1024 * 1024

bf16 = jnp.bfloat16
f32 = jnp.float32


def in_vmem():
    return pl.BlockSpec(memory_space=pltpu.VMEM)


def in_smem():
    return pl.BlockSpec(memory_space=pltpu.SMEM)


def in_hbm():
    return pl.BlockSpec(memory_space=pltpu.HBM)


def anywhere():
    return pl.BlockSpec(memory_space=pl.ANY)


def params():
    return pltpu.CompilerParams(vmem_limit_bytes=VMEM_LIMIT)


def cost(flops, moved, transcendentals=0):
    return pl.CostEstimate(
        flops=int(flops), bytes_accessed=int(moved), transcendentals=int(transcendentals)
    )


def rms_norm(rows, gain):
    widened = rows.astype(f32)
    scaling = lax.rsqrt(jnp.mean(widened * widened, axis=1, keepdims=True) + 1e-06)
    return (widened * scaling * gain).astype(bf16)


def dot32(left, right):
    return jnp.dot(left, right, preferred_element_type=f32)


def packed_places(dest_ref, clusters, lanes, slots, counts):
    me = lax.axis_index("ball")
    capacity = 2 * clusters // lanes
    offsets = []
    for offset in range(lanes):
        slots[offset] = 0
        counts[offset] = 0
    for cluster in range(clusters):
        offset = lax.rem(dest_ref[cluster] // clusters - me + lanes, lanes)
        slots[offset] = 1
        offsets.append(offset)
    if capacity * 2 == clusters:
        low, high = offsets[0], offsets[0]
        for offset in offsets[1:]:
            low, high = jnp.minimum(low, offset), jnp.maximum(high, offset)
        swap = high - low > lanes // 2
        slots[low] = jnp.where(swap, 1, 0)
        slots[high] = jnp.where(swap, 0, 1)
        across = high - low == lanes // 2
    else:
        taken = 0
        for offset in range(lanes):
            here = slots[offset]
            slots[offset] = taken
            taken = taken + here
        across = None
    places = []
    for offset in offsets:
        rank = counts[offset]
        counts[offset] = rank + 1
        place = (slots[offset] * capacity + rank) * CLUSTER
        places.append(pl.multiple_of(place, CLUSTER))
    return places, across


def factor_of(head_size):
    return math.log2(math.e) / math.sqrt(head_size)


def extended_values(values, head_size):
    columns, rows = values.shape[1], values.shape[0]
    turned = values.T
    ones = jnp.ones((16, rows), bf16)
    return [
        jnp.concatenate([turned[h * head_size : (h + 1) * head_size], ones], axis=0)
        for h in range(columns // head_size)
    ]


def masked_query(query, head, head_size):
    row = lax.broadcasted_iota(jnp.int32, (TILE, 1), 0) // head_size
    return jnp.where(row == head % (TILE // head_size), query, bf16(0))


def run_jobs(jobs, ahead=AHEAD):
    waiting = [first() for first, _ in jobs[:ahead]]
    for index, (_, second) in enumerate(jobs):
        if index + ahead < len(jobs):
            waiting.append(jobs[index + ahead][0]())
        second(waiting.pop(0))


def plain_weights(scores, head_size):
    return jnp.exp2(scores * factor_of(head_size)).astype(bf16)


def attention_jobs(qt_ref, columns_of_query, heads, parts_of, head_size, store):
    per_tile = TILE // head_size
    kept = head_size + 8
    sums = {}
    jobs = []

    def job(start, head, key_ref, value_ref, first, last):
        tile = slice(head // per_tile * TILE, (head // per_tile + 1) * TILE)
        queries = slice(start, start + QUERY_BLOCK)
        rows = slice(first, first + KEY_BLOCK)

        def scores():
            query = masked_query(qt_ref[tile, queries], head, head_size)
            return dot32(key_ref[rows, tile], query)

        def mix(values):
            mixed = dot32(value_ref[head, :, rows], plain_weights(values, head_size))[:kept]
            if (start, head) in sums:
                mixed = mixed + sums.pop((start, head))
            if last:
                store(head, queries, mixed)
            else:
                sums[start, head] = mixed

        return scores, mix

    for start in columns_of_query:
        for head in heads:
            blocks = [
                (keys, values, row)
                for keys, values, first, end in parts_of(start)
                for row in range(first, end, KEY_BLOCK)
            ]
            for index, (keys, values, row) in enumerate(blocks):
                jobs.append(job(start, head, keys, values, row, index + 1 == len(blocks)))
    return jobs


def divided(sums, head_size):
    return (sums[:head_size] / sums[head_size : head_size + 1]).astype(bf16)


def head_norms(rows, head_size):
    columns = rows.shape[1]
    widened = rows.astype(f32)
    channel = lax.broadcasted_iota(jnp.int32, (columns, TILE), 0) // head_size
    head = lax.broadcasted_iota(jnp.int32, (columns, TILE), 1)
    members = (channel == head).astype(bf16)
    return jnp.max(dot32((widened * widened).astype(bf16), members), axis=0, keepdims=True)


def exponents_safe(query_norms, key_norms, head_size):
    limit = (SAFE_EXPONENT / factor_of(head_size)) ** 2
    return jnp.max(query_norms * key_norms) <= limit


def shifted_attention(qt_ref, start, count, parts, head_size, out_ref):
    per_tile = TILE // head_size

    def step(index, carry):
        head = index % HEADS
        block = pl.multiple_of(start + index // HEADS * SLOW_BLOCK, SLOW_BLOCK)
        tile = pl.multiple_of(head // per_tile * TILE, TILE)
        query = masked_query(
            qt_ref[pl.ds(tile, TILE), pl.ds(block, SLOW_BLOCK)], head, head_size
        )
        loaded = [part(pl.ds(tile, TILE), head) for part in parts]
        scores = [dot32(keys, query) for keys, _ in loaded]
        top = jnp.max(scores[0], axis=0, keepdims=True)
        for more in scores[1:]:
            top = jnp.maximum(top, jnp.max(more, axis=0, keepdims=True))
        mixed = 0.0
        for block_scores, (_, values) in zip(scores, loaded):
            mixed = mixed + dot32(values, plain_weights(block_scores - top, head_size))
        rows = pl.ds(pl.multiple_of(head * head_size, head_size), head_size)
        out_ref[rows, pl.ds(block, SLOW_BLOCK)] = (
            mixed[:head_size] / mixed[head_size : head_size + 1]
        ).astype(bf16)
        return carry

    lax.fori_loop(0, HEADS * (count // SLOW_BLOCK), step, 0)


def gelu(value):
    slope = math.sqrt(2.0 / math.pi)
    inner = value * (value * value * (0.044715 * slope) + slope)
    half = 0.5 * value
    return half + half * jnp.tanh(inner)


def pack_kernel(
    lanes, clusters, dest_hbm, points_ref, gain_first, gain_second, packed_ref, first_ref,
    second_ref, dest_ref, dest, slots, counts, sems,
):
    fetch = pltpu.make_async_copy(dest_hbm, dest, sems.at[clusters])
    fetch.start()
    moved = [
        pltpu.make_async_copy(gain_first, first_ref, sems.at[clusters + 1]),
        pltpu.make_async_copy(gain_second, second_ref, sems.at[clusters + 2]),
        pltpu.make_async_copy(dest_hbm, dest_ref, sems.at[clusters + 3]),
    ]
    for copy in moved:
        copy.start()
    fetch.wait()
    places, _ = packed_places(dest, clusters, lanes, slots, counts)
    copies = [
        pltpu.make_async_copy(
            points_ref.at[pl.ds(cluster * CLUSTER, CLUSTER)],
            packed_ref.at[pl.ds(place, CLUSTER)],
            sems.at[cluster],
        )
        for cluster, place in enumerate(places)
    ]
    for copy in copies:
        copy.start()
    for copy in moved + copies:
        copy.wait()


def project_kernel(
    head_size, packed_ref, gain_ref, wqk_ref, wv_ref, qt_ref, k_ref, vt_ref, pool_ref, facts_ref
):
    rows, columns = packed_ref.shape
    normed = rms_norm(packed_ref[...], gain_ref[...])
    paired = dot32(normed, wqk_ref[...]).astype(bf16)
    values = dot32(normed, wv_ref[...]).astype(bf16)
    query, keys = paired[:, :columns], paired[:, columns:]
    k_ref[...] = keys
    pooled = rows // POOL
    row = lax.broadcasted_iota(jnp.int32, (pooled, rows), 0)
    column = lax.broadcasted_iota(jnp.int32, (pooled, rows), 1)
    averaging = jnp.where(column // POOL == row, 1.0 / math.sqrt(POOL), 0.0).astype(bf16)
    pool_ref[:pooled] = dot32(averaging, keys).astype(bf16)
    pool_ref[pooled:] = dot32(averaging, values).astype(bf16)
    qt_ref[...] = query.T
    for head, extended in enumerate(extended_values(values, head_size)):
        vt_ref[head] = extended
    facts_ref[0:1] = head_norms(query, head_size)
    facts_ref[1:2] = head_norms(keys, head_size)


def near_part_kernel(heads, head_size, qt_ref, k_ref, vt_ref, o_ref):
    rows = k_ref.shape[0]

    def store(head, queries, sums):
        o_ref[head - heads[0], :, queries] = sums

    run_jobs(
        attention_jobs(
            qt_ref,
            range(0, rows, QUERY_BLOCK),
            heads,
            lambda start: [(k_ref, vt_ref, 0, rows)],
            head_size,
            store,
        )
    )


def near_kernel(head_size, qt_ref, k_ref, vt_ref, facts_ref, pool_ref, *rest):
    partial = [(ref, inner) for ref in rest[:-3] for inner in range(ref.shape[0])]
    y_ref, kp_ref, vp_ref = rest[-3:]
    rows = k_ref.shape[0]
    regions, pooled = pool_ref.shape[0], pool_ref.shape[1] // 2
    for region in range(regions):
        kp_ref[region * pooled : (region + 1) * pooled] = pool_ref[region, :pooled]
    gathered = jnp.concatenate([pool_ref[r, pooled:] for r in range(regions)], axis=0)
    for head, extended in enumerate(extended_values(gathered, head_size)):
        vp_ref[head] = extended
    key_norms = jnp.maximum(facts_ref[1:2], head_norms(kp_ref[...], head_size))
    safe = exponents_safe(facts_ref[0:1], key_norms, head_size)

    def store(head, queries, sums):
        ref, inner = partial[head]
        sums = sums + ref[inner, :, queries]
        y_ref[head * head_size : (head + 1) * head_size, queries] = divided(sums, head_size)

    run_jobs(
        attention_jobs(
            qt_ref,
            range(0, rows, QUERY_BLOCK),
            range(HEADS),
            lambda start: [(kp_ref, vp_ref, 0, regions * pooled)],
            head_size,
            store,
        )
    )

    @pl.when(jnp.logical_not(safe))
    def _():
        shifted_attention(
            qt_ref,
            0,
            rows,
            [
                lambda tile, head: (k_ref[:, tile], vt_ref[head]),
                lambda tile, head: (kp_ref[:, tile], vp_ref[head]),
            ],
            head_size,
            y_ref,
        )


class OutputRows:
    def __init__(
        self, places, points_ref, near_ref, far_ref, wo_ref, gain_ref, up_ref, down_ref, out_ref,
        done_ref, origin, sems,
    ):
        for cluster, place in enumerate(places):
            origin[place // CLUSTER] = cluster
        self.refs = points_ref, near_ref, far_ref, wo_ref, gain_ref, up_ref, down_ref
        self.out_ref, self.done_ref, self.origin, self.sems = out_ref, done_ref, origin, sems
        self.rows = points_ref.shape[0]

    def back(self, slot):
        target = pl.multiple_of(self.origin[slot] * CLUSTER, CLUSTER)
        return pltpu.make_async_copy(
            self.done_ref.at[pl.ds(slot * CLUSTER, CLUSTER)],
            self.out_ref.at[pl.ds(target, CLUSTER)],
            self.sems.at[slot],
        )

    def job(self, start):
        points_ref, near_ref, far_ref, wo_ref, gain_ref, up_ref, down_ref = self.refs
        block = slice(start, start + ROW_BLOCK)

        def widen():
            after = (
                points_ref[block].astype(f32)
                + dot32(near_ref[:, block].T, wo_ref[...])
                + dot32(far_ref[:, block].T, wo_ref[...])
            ).astype(bf16)
            return after, dot32(rms_norm(after, gain_ref[...]), up_ref[...])

        def narrow(widened):
            after, hidden = widened
            hidden = gelu(hidden).astype(bf16)
            self.done_ref[block] = (after.astype(f32) + dot32(hidden, down_ref[...])).astype(bf16)
            for slot in range(start // CLUSTER, (start + ROW_BLOCK) // CLUSTER):
                self.back(slot).start()

        return widen, narrow

    def jobs(self, first, end):
        return [self.job(start) for start in range(first, end, ROW_BLOCK)]

    def wait(self):
        for slot in range(self.rows // CLUSTER):
            self.back(slot).wait()


def far_finish_kernel(
    lanes, clusters, head_size, dest_ref, points_ref, near_ref, next_ref, prior_ref, across_ref,
    qt_ref, k_ref, vt_ref, facts_ref, gain_ref, gain_second, wqk_ref, wv_ref, wo_ref, up_ref,
    down_ref, out_ref, kr_ref, vr_ref, y_ref, done_ref, slots, counts, origin, sems,
):
    places, across = packed_places(dest_ref, clusters, lanes, slots, counts)
    output = OutputRows(
        places, points_ref, near_ref, y_ref, wo_ref, gain_second, up_ref, down_ref, out_ref,
        done_ref, origin, sems,
    )
    rows, columns = k_ref.shape
    half = rows // 2
    found = {}

    def prepare(_):
        apart = jnp.concatenate([next_ref[...], prior_ref[...]], axis=0)
        normed = rms_norm(jnp.where(across, across_ref[...], apart), gain_ref[...])
        keys = dot32(normed, wqk_ref[:, columns:]).astype(bf16)
        values = dot32(normed, wv_ref[...]).astype(bf16)
        kr_ref[...] = keys
        for head, extended in enumerate(extended_values(values, head_size)):
            vr_ref[head] = extended
        key_norms = jnp.maximum(facts_ref[1:2], head_norms(keys, head_size))
        found["safe"] = exponents_safe(facts_ref[0:1], key_norms, head_size)

    def keep(head, queries, sums):
        found[head, queries.start] = sums

    def store(head, queries, sums):
        sums = sums + found.pop((head, queries.start))
        y_ref[head * head_size : (head + 1) * head_size, queries] = divided(sums, head_size)

    def own_part(start):
        mine = start // half * half
        return [(k_ref, vt_ref, mine, mine + half)]

    def arrived_part(start):
        other = half - start // half * half
        return [(kr_ref, vr_ref, other, other + half)]

    def attend(parts_of, finish):
        return attention_jobs(
            qt_ref, range(0, rows, QUERY_BLOCK), range(HEADS), parts_of, head_size, finish
        )

    jobs = attend(own_part, keep)
    jobs.insert(PREPARE_AFTER, (lambda: None, prepare))
    run_jobs(jobs + attend(arrived_part, store))
    safe = found["safe"]
    run_jobs(output.jobs(0, rows), ahead=1)
    output.wait()

    @pl.when(jnp.logical_not(safe))
    def _():
        for start in (0, half):
            mine, other = slice(start, start + half), slice(half - start, rows - start)
            shifted_attention(
                qt_ref,
                start,
                half,
                [
                    lambda tile, head, mine=mine: (k_ref[mine, tile], vt_ref[head, :, mine]),
                    lambda tile, head, other=other: (kr_ref[other, tile], vr_ref[head, :, other]),
                ],
                head_size,
                y_ref,
            )
        run_jobs(output.jobs(0, rows), ahead=1)
        output.wait()


def finish_kernel(
    lanes, clusters, dest_ref, points_ref, near_ref, far_ref, wo_ref, gain_ref, up_ref, down_ref,
    out_ref, done_ref, slots, counts, origin, sems,
):
    places, _ = packed_places(dest_ref, clusters, lanes, slots, counts)
    output = OutputRows(
        places, points_ref, near_ref, far_ref, wo_ref, gain_ref, up_ref, down_ref, out_ref,
        done_ref, origin, sems,
    )
    run_jobs(output.jobs(0, output.rows), ahead=1)
    output.wait()


def owner_far_kernel(head_size, x_ref, gain_ref, wqk_ref, wv_ref, out_ref, qt, k, vt, y):
    rows, columns = x_ref.shape
    normed = rms_norm(x_ref[...], gain_ref[...])
    paired = dot32(normed, wqk_ref[...]).astype(bf16)
    values = dot32(normed, wv_ref[...]).astype(bf16)
    qt[...] = paired[:, :columns].T
    k[...] = paired[:, columns:]
    for head, extended in enumerate(extended_values(values, head_size)):
        vt[head] = extended
    shifted_attention(
        qt, 0, rows, [lambda tile, head: (k[:, tile], vt[head])], head_size, y
    )
    out_ref[...] = y[...].T


def per_device(
    points, gain_attn, w_query_key, w_value, w_out, gain_mlp, w_up, w_down, cluster_dest
):
    columns = points.shape[-1]
    flat = points.reshape(-1, columns)
    rows = flat.shape[0]
    lanes, regions = lax.axis_size("ball"), lax.axis_size("region")
    clusters = rows // CLUSTER
    share = 2 * clusters // lanes * CLUSTER
    owners = rows // share
    pooled = rows // POOL
    head_size = columns // HEADS
    tall = head_size + 16
    kept = head_size + 8
    dest = cluster_dest.reshape(clusters)
    gain_first = gain_attn.reshape(1, columns)
    gain_second = gain_mlp.reshape(1, columns)
    wide = jax.ShapeDtypeStruct((rows, columns), bf16)
    turned = jax.ShapeDtypeStruct((columns, rows), bf16)
    extended = jax.ShapeDtypeStruct((HEADS, tall, rows), bf16)
    scalars = [pltpu.SMEM((lanes,), jnp.int32)] * 2

    def attention_cost(queries, keys, heads):
        return cost(3 * heads * queries * keys * 256, 4 * rows * columns, heads * queries * keys)

    def shift(data, offset):
        return lax.ppermute(data, "ball", [(i, (i + offset) % lanes) for i in range(lanes)])

    row_of_gains = jax.ShapeDtypeStruct((1, columns), f32)
    packed, gain_first, gain_second, dest = pl.pallas_call(
        functools.partial(pack_kernel, lanes, clusters),
        out_shape=[wide, row_of_gains, row_of_gains, jax.ShapeDtypeStruct(dest.shape, jnp.int32)],
        in_specs=[in_hbm()] * 4,
        out_specs=[anywhere()] * 4,
        scratch_shapes=[pltpu.SMEM((clusters,), jnp.int32)]
        + scalars
        + [pltpu.SemaphoreType.DMA((clusters + 4,))],
        cost_estimate=cost(0, 4 * rows * columns),
        compiler_params=params(),
        name="pack",
    )(
        *(
            pltpu.with_memory_space_constraint(held, pltpu.HBM)
            for held in (dest, flat, gain_first, gain_second)
        )
    )

    pair_path = owners == 2 and lanes == 4
    if pair_path:
        from_across = shift(packed, 2)
        from_next = shift(packed[:share], lanes - 1)
        from_prior = shift(packed[share:], 1)

    query, keys, values, pool, facts = pl.pallas_call(
        functools.partial(project_kernel, head_size),
        out_shape=[
            turned,
            wide,
            extended,
            jax.ShapeDtypeStruct((2 * pooled, columns), bf16),
            jax.ShapeDtypeStruct((8, TILE), f32),
        ],
        in_specs=[in_vmem()] * 4,
        out_specs=[in_vmem()] * 5,
        cost_estimate=cost(6 * rows * columns * columns, 10 * rows * columns),
        compiler_params=params(),
        name="project",
    )(packed, gain_first, w_query_key, w_value)

    def across_regions(data, mask):
        return lax.ppermute(data, "region", [(i, i ^ mask) for i in range(regions)])

    gathered = pool.reshape(1, 2 * pooled, columns)
    step = regions // 2
    while step:
        gathered = jnp.concatenate([gathered, across_regions(gathered, step)], axis=0)
        step //= 2
    partial = [
        pl.pallas_call(
            functools.partial(near_part_kernel, heads, head_size),
            out_shape=jax.ShapeDtypeStruct((len(heads), kept, rows), f32),
            in_specs=[in_vmem()] * 3,
            out_specs=in_vmem(),
            cost_estimate=attention_cost(rows, rows, HEADS // 2),
            compiler_params=params(),
            name="near_part",
        )(query, keys, values)
        for heads in (range(FIRST_HEADS), range(FIRST_HEADS, HEADS))
    ]

    near = pl.pallas_call(
        functools.partial(near_kernel, head_size),
        out_shape=turned,
        in_specs=[in_vmem()] * (5 + len(partial)),
        out_specs=in_vmem(),
        scratch_shapes=[
            pltpu.VMEM((regions * pooled, columns), bf16),
            pltpu.VMEM((HEADS, tall, regions * pooled), bf16),
        ],
        cost_estimate=attention_cost(rows, regions * pooled, HEADS),
        compiler_params=params(),
        name="near",
    )(query, keys, values, facts, gathered, *partial)

    last_scratch = (
        [pltpu.VMEM((rows, columns), bf16)]
        + scalars
        + [pltpu.SMEM((clusters,), jnp.int32), pltpu.SemaphoreType.DMA((clusters,))]
    )
    if pair_path:
        block_out = pl.pallas_call(
            functools.partial(far_finish_kernel, lanes, clusters, head_size),
            out_shape=wide,
            in_specs=[in_smem()] + [in_vmem()] * 16,
            out_specs=anywhere(),
            scratch_shapes=[
                pltpu.VMEM((rows, columns), bf16),
                pltpu.VMEM((HEADS, tall, rows), bf16),
                pltpu.VMEM((columns, rows), bf16),
            ]
            + last_scratch,
            cost_estimate=attention_cost(rows, rows, HEADS),
            compiler_params=params(),
            name="far_finish",
        )(
            dest, packed, near, from_next, from_prior, from_across, query, keys, values, facts,
            gain_first, gain_second, w_query_key, w_value, w_out, w_up, w_down,
        )
    else:
        targets = dest // clusters
        members = lax.rem(targets - lax.axis_index("ball") + lanes, lanes)
        present = jnp.zeros((lanes,), jnp.int32).at[members].set(1)
        slot = jnp.cumsum(present) - present
        blocks = packed.reshape(owners, share, columns)
        empty = jnp.zeros((owners, share, columns), bf16)
        arrived, back = empty, empty

        def picked(source, offset):
            return lax.dynamic_index_in_dim(source, jnp.minimum(slot[offset], owners - 1), 0, False)

        def put(target, offset, block):
            index = jnp.minimum(slot[offset], owners - 1)
            placed = lax.dynamic_update_index_in_dim(target, block, index, 0)
            return jnp.where(present[offset] == 1, placed, target)

        for offset in range(lanes):
            block = picked(blocks, offset)
            arrived = put(arrived, offset, shift(block, offset) if offset else block)
        far_rotated = pl.pallas_call(
            functools.partial(owner_far_kernel, head_size),
            out_shape=wide,
            in_specs=[in_vmem()] * 4,
            out_specs=in_vmem(),
            scratch_shapes=[
                pltpu.VMEM((columns, rows), bf16),
                pltpu.VMEM((rows, columns), bf16),
                pltpu.VMEM((HEADS, tall, rows), bf16),
                pltpu.VMEM((columns, rows), bf16),
            ],
            cost_estimate=attention_cost(rows, rows, HEADS),
            compiler_params=params(),
            name="owner_far",
        )(arrived.reshape(rows, columns), gain_first, w_query_key, w_value)
        leaving = far_rotated.reshape(owners, share, columns)
        for offset in range(lanes):
            block = picked(leaving, offset)
            back = put(back, offset, shift(block, lanes - offset) if offset else block)
        block_out = pl.pallas_call(
            functools.partial(finish_kernel, lanes, clusters),
            out_shape=wide,
            in_specs=[in_smem()] + [in_vmem()] * 7,
            out_specs=anywhere(),
            scratch_shapes=last_scratch,
            cost_estimate=cost(20 * rows * columns * columns, 8 * rows * columns),
            compiler_params=params(),
            name="finish",
        )(
            dest, packed, near, back.reshape(rows, columns).T, w_out, gain_second, w_up, w_down
        )
    return block_out.reshape(points.shape)


def solution(mesh):
    placed = (
        P("ball", "region", None, None),
        P(),
        P(),
        P(),
        P(),
        P(),
        P(),
        P(),
        P("ball", "region", None),
    )
    return jax.shard_map(
        per_device,
        mesh=mesh,
        in_specs=placed,
        out_specs=P("ball", "region", None, None),
        check_vma=False,
    )
```

```python
import functools
import math

import jax
import jax.numpy as jnp
from jax import lax
from jax.experimental import pallas as pl
from jax.experimental.pallas import tpu as pltpu
from jax.sharding import PartitionSpec as P

HEADS = 8
CLUSTER = 64
POOL = 16
TILE = 128
SLOW_BLOCK = 256
QUERY_BLOCK = 512
KEY_BLOCK = 256
AHEAD = 2
PREPARE_AFTER = 4
FIRST_HEADS = 6
ROW_BLOCK = 256
SAFE_EXPONENT = 104.0
VMEM_LIMIT = 48 * 1024 * 1024

bf16 = jnp.bfloat16
f32 = jnp.float32


def in_vmem():
    return pl.BlockSpec(memory_space=pltpu.VMEM)


def in_smem():
    return pl.BlockSpec(memory_space=pltpu.SMEM)


def in_hbm():
    return pl.BlockSpec(memory_space=pltpu.HBM)


def anywhere():
    return pl.BlockSpec(memory_space=pl.ANY)


def params():
    return pltpu.CompilerParams(vmem_limit_bytes=VMEM_LIMIT)


def cost(flops, moved, transcendentals=0):
    return pl.CostEstimate(
        flops=int(flops), bytes_accessed=int(moved), transcendentals=int(transcendentals)
    )


def rms_norm(rows, gain):
    widened = rows.astype(f32)
    scaling = lax.rsqrt(jnp.mean(widened * widened, axis=1, keepdims=True) + 1e-06)
    return (widened * scaling * gain).astype(bf16)


def dot32(left, right):
    return jnp.dot(left, right, preferred_element_type=f32)


def packed_places(dest_ref, clusters, lanes, slots, counts):
    me = lax.axis_index("ball")
    capacity = 2 * clusters // lanes
    offsets = []
    for offset in range(lanes):
        slots[offset] = 0
        counts[offset] = 0
    for cluster in range(clusters):
        if clusters & (clusters - 1) or lanes & (lanes - 1):
            offset = lax.rem(dest_ref[cluster] // clusters - me + lanes, lanes)
        else:
            owner = lax.shift_right_logical(dest_ref[cluster], clusters.bit_length() - 1)
            offset = (owner - me + lanes) & (lanes - 1)
        slots[offset] = 1
        offsets.append(offset)
    if capacity * 2 == clusters:
        low, high = offsets[0], offsets[0]
        for offset in offsets[1:]:
            low, high = jnp.minimum(low, offset), jnp.maximum(high, offset)
        swap = high - low > lanes // 2
        slots[low] = jnp.where(swap, 1, 0)
        slots[high] = jnp.where(swap, 0, 1)
        across = high - low == lanes // 2
    else:
        taken = 0
        for offset in range(lanes):
            here = slots[offset]
            slots[offset] = taken
            taken = taken + here
        across = None
    places = []
    for offset in offsets:
        rank = counts[offset]
        counts[offset] = rank + 1
        place = (slots[offset] * capacity + rank) * CLUSTER
        places.append(pl.multiple_of(place, CLUSTER))
    return places, across


def factor_of(head_size):
    return math.log2(math.e) / math.sqrt(head_size)


def extended_values(values, head_size):
    columns, rows = values.shape[1], values.shape[0]
    turned = values.T
    ones = jnp.ones((16, rows), bf16)
    return [
        jnp.concatenate([turned[h * head_size : (h + 1) * head_size], ones], axis=0)
        for h in range(columns // head_size)
    ]


def masked_query(query, head, head_size):
    row = lax.broadcasted_iota(jnp.int32, (TILE, 1), 0) // head_size
    return jnp.where(row == head % (TILE // head_size), query, bf16(0))


def run_jobs(jobs, ahead=AHEAD):
    waiting = [first() for first, _ in jobs[:ahead]]
    for index, (_, second) in enumerate(jobs):
        if index + ahead < len(jobs):
            waiting.append(jobs[index + ahead][0]())
        second(waiting.pop(0))


def plain_weights(scores, head_size):
    return jnp.exp2(scores * factor_of(head_size)).astype(bf16)


def attention_jobs(qt_ref, columns_of_query, heads, parts_of, head_size, store):
    per_tile = TILE // head_size
    kept = head_size + 8
    sums = {}
    jobs = []

    def job(start, head, key_ref, value_ref, first, last):
        tile = slice(head // per_tile * TILE, (head // per_tile + 1) * TILE)
        queries = slice(start, start + QUERY_BLOCK)
        rows = slice(first, first + KEY_BLOCK)

        def scores():
            query = masked_query(qt_ref[tile, queries], head, head_size)
            return dot32(key_ref[rows, tile], query)

        def mix(values):
            mixed = dot32(value_ref[head, :, rows], plain_weights(values, head_size))[:kept]
            if (start, head) in sums:
                mixed = mixed + sums.pop((start, head))
            if last:
                store(head, queries, mixed)
            else:
                sums[start, head] = mixed

        return scores, mix

    for start in columns_of_query:
        for head in heads:
            blocks = [
                (keys, values, row)
                for keys, values, first, end in parts_of(start)
                for row in range(first, end, KEY_BLOCK)
            ]
            for index, (keys, values, row) in enumerate(blocks):
                jobs.append(job(start, head, keys, values, row, index + 1 == len(blocks)))
    return jobs


def divided(sums, head_size):
    return (sums[:head_size] / sums[head_size : head_size + 1]).astype(bf16)


def head_norms(rows, head_size):
    columns = rows.shape[1]
    widened = rows.astype(f32)
    channel = lax.broadcasted_iota(jnp.int32, (columns, TILE), 0) // head_size
    head = lax.broadcasted_iota(jnp.int32, (columns, TILE), 1)
    members = (channel == head).astype(bf16)
    return jnp.max(dot32((widened * widened).astype(bf16), members), axis=0, keepdims=True)


def exponents_safe(query_norms, key_norms, head_size):
    limit = (SAFE_EXPONENT / factor_of(head_size)) ** 2
    return jnp.max(query_norms * key_norms) <= limit


def shifted_attention(qt_ref, start, count, parts, head_size, out_ref):
    per_tile = TILE // head_size

    def step(index, carry):
        head = index % HEADS
        block = pl.multiple_of(start + index // HEADS * SLOW_BLOCK, SLOW_BLOCK)
        tile = pl.multiple_of(head // per_tile * TILE, TILE)
        query = masked_query(
            qt_ref[pl.ds(tile, TILE), pl.ds(block, SLOW_BLOCK)], head, head_size
        )
        loaded = [part(pl.ds(tile, TILE), head) for part in parts]
        scores = [dot32(keys, query) for keys, _ in loaded]
        top = jnp.max(scores[0], axis=0, keepdims=True)
        for more in scores[1:]:
            top = jnp.maximum(top, jnp.max(more, axis=0, keepdims=True))
        mixed = 0.0
        for block_scores, (_, values) in zip(scores, loaded):
            mixed = mixed + dot32(values, plain_weights(block_scores - top, head_size))
        rows = pl.ds(pl.multiple_of(head * head_size, head_size), head_size)
        out_ref[rows, pl.ds(block, SLOW_BLOCK)] = (
            mixed[:head_size] / mixed[head_size : head_size + 1]
        ).astype(bf16)
        return carry

    lax.fori_loop(0, HEADS * (count // SLOW_BLOCK), step, 0)


def gelu(value):
    slope = math.sqrt(2.0 / math.pi)
    inner = value * (value * value * (0.044715 * slope) + slope)
    half = 0.5 * value
    return half + half * jnp.tanh(inner)


def pack_kernel(
    lanes, clusters, dest_hbm, points_ref, gain_first, gain_second, packed_ref, first_ref,
    second_ref, dest_ref, dest, slots, counts, sems,
):
    fetch = pltpu.make_async_copy(dest_hbm, dest, sems.at[clusters])
    fetch.start()
    moved = [
        pltpu.make_async_copy(gain_first, first_ref, sems.at[clusters + 1]),
        pltpu.make_async_copy(gain_second, second_ref, sems.at[clusters + 2]),
        pltpu.make_async_copy(dest_hbm, dest_ref, sems.at[clusters + 3]),
    ]
    for copy in moved:
        copy.start()
    fetch.wait()
    places, _ = packed_places(dest, clusters, lanes, slots, counts)
    copies = [
        pltpu.make_async_copy(
            points_ref.at[pl.ds(cluster * CLUSTER, CLUSTER)],
            packed_ref.at[pl.ds(place, CLUSTER)],
            sems.at[cluster],
        )
        for cluster, place in enumerate(places)
    ]
    for copy in copies:
        copy.start()
    for copy in moved + copies:
        copy.wait()


def project_kernel(
    head_size, packed_ref, gain_ref, wqk_ref, wv_ref, qt_ref, k_ref, vt_ref, pool_ref, facts_ref
):
    rows, columns = packed_ref.shape
    normed = rms_norm(packed_ref[...], gain_ref[...])
    paired = dot32(normed, wqk_ref[...]).astype(bf16)
    values = dot32(normed, wv_ref[...]).astype(bf16)
    query, keys = paired[:, :columns], paired[:, columns:]
    k_ref[...] = keys
    pooled = rows // POOL
    row = lax.broadcasted_iota(jnp.int32, (pooled, rows), 0)
    column = lax.broadcasted_iota(jnp.int32, (pooled, rows), 1)
    averaging = jnp.where(column // POOL == row, 1.0 / math.sqrt(POOL), 0.0).astype(bf16)
    pool_ref[:pooled] = dot32(averaging, keys).astype(bf16)
    pool_ref[pooled:] = dot32(averaging, values).astype(bf16)
    qt_ref[...] = query.T
    for head, extended in enumerate(extended_values(values, head_size)):
        vt_ref[head] = extended
    facts_ref[0:1] = head_norms(query, head_size)
    facts_ref[1:2] = head_norms(keys, head_size)


def near_part_kernel(heads, head_size, qt_ref, k_ref, vt_ref, o_ref):
    rows = k_ref.shape[0]

    def store(head, queries, sums):
        o_ref[head - heads[0], :, queries] = sums

    run_jobs(
        attention_jobs(
            qt_ref,
            range(0, rows, QUERY_BLOCK),
            heads,
            lambda start: [(k_ref, vt_ref, 0, rows)],
            head_size,
            store,
        )
    )


def near_kernel(head_size, qt_ref, k_ref, vt_ref, facts_ref, pool_ref, *rest):
    partial = [(ref, inner) for ref in rest[:-3] for inner in range(ref.shape[0])]
    y_ref, kp_ref, vp_ref = rest[-3:]
    rows = k_ref.shape[0]
    regions, pooled = pool_ref.shape[0], pool_ref.shape[1] // 2
    for region in range(regions):
        kp_ref[region * pooled : (region + 1) * pooled] = pool_ref[region, :pooled]
    gathered = jnp.concatenate([pool_ref[r, pooled:] for r in range(regions)], axis=0)
    for head, extended in enumerate(extended_values(gathered, head_size)):
        vp_ref[head] = extended
    key_norms = jnp.maximum(facts_ref[1:2], head_norms(kp_ref[...], head_size))
    safe = exponents_safe(facts_ref[0:1], key_norms, head_size)

    def store(head, queries, sums):
        ref, inner = partial[head]
        sums = sums + ref[inner, :, queries]
        y_ref[head * head_size : (head + 1) * head_size, queries] = divided(sums, head_size)

    run_jobs(
        attention_jobs(
            qt_ref,
            range(0, rows, QUERY_BLOCK),
            range(HEADS),
            lambda start: [(kp_ref, vp_ref, 0, regions * pooled)],
            head_size,
            store,
        )
    )

    @pl.when(jnp.logical_not(safe))
    def _():
        shifted_attention(
            qt_ref,
            0,
            rows,
            [
                lambda tile, head: (k_ref[:, tile], vt_ref[head]),
                lambda tile, head: (kp_ref[:, tile], vp_ref[head]),
            ],
            head_size,
            y_ref,
        )


class OutputRows:
    def __init__(
        self, places, points_ref, near_ref, far_ref, wo_ref, gain_ref, up_ref, down_ref, out_ref,
        done_ref, origin, sems,
    ):
        for cluster, place in enumerate(places):
            origin[place // CLUSTER] = cluster
        self.refs = points_ref, near_ref, far_ref, wo_ref, gain_ref, up_ref, down_ref
        self.out_ref, self.done_ref, self.origin, self.sems = out_ref, done_ref, origin, sems
        self.rows = points_ref.shape[0]

    def back(self, slot):
        target = pl.multiple_of(self.origin[slot] * CLUSTER, CLUSTER)
        return pltpu.make_async_copy(
            self.done_ref.at[pl.ds(slot * CLUSTER, CLUSTER)],
            self.out_ref.at[pl.ds(target, CLUSTER)],
            self.sems.at[slot],
        )

    def job(self, start):
        points_ref, near_ref, far_ref, wo_ref, gain_ref, up_ref, down_ref = self.refs
        block = slice(start, start + ROW_BLOCK)

        def widen():
            after = (
                points_ref[block].astype(f32)
                + dot32(near_ref[:, block].T, wo_ref[...])
                + dot32(far_ref[:, block].T, wo_ref[...])
            ).astype(bf16)
            return after, dot32(rms_norm(after, gain_ref[...]), up_ref[...])

        def narrow(widened):
            after, hidden = widened
            hidden = gelu(hidden).astype(bf16)
            self.done_ref[block] = (after.astype(f32) + dot32(hidden, down_ref[...])).astype(bf16)
            for slot in range(start // CLUSTER, (start + ROW_BLOCK) // CLUSTER):
                self.back(slot).start()

        return widen, narrow

    def jobs(self, first, end):
        return [self.job(start) for start in range(first, end, ROW_BLOCK)]

    def wait(self):
        for slot in range(self.rows // CLUSTER):
            self.back(slot).wait()


def far_finish_kernel(
    lanes, clusters, head_size, dest_ref, points_ref, near_ref, next_ref, prior_ref, across_ref,
    qt_ref, k_ref, vt_ref, facts_ref, gain_ref, gain_second, wqk_ref, wv_ref, wo_ref, up_ref,
    down_ref, out_ref, kr_ref, vr_ref, y_ref, done_ref, slots, counts, origin, sems,
):
    places, across = packed_places(dest_ref, clusters, lanes, slots, counts)
    output = OutputRows(
        places, points_ref, near_ref, y_ref, wo_ref, gain_second, up_ref, down_ref, out_ref,
        done_ref, origin, sems,
    )
    rows, columns = k_ref.shape
    half = rows // 2
    found = {}

    def prepare(_):
        apart = jnp.concatenate([next_ref[...], prior_ref[...]], axis=0)
        normed = rms_norm(jnp.where(across, across_ref[...], apart), gain_ref[...])
        keys = dot32(normed, wqk_ref[:, columns:]).astype(bf16)
        values = dot32(normed, wv_ref[...]).astype(bf16)
        kr_ref[...] = keys
        for head, extended in enumerate(extended_values(values, head_size)):
            vr_ref[head] = extended
        key_norms = jnp.maximum(facts_ref[1:2], head_norms(keys, head_size))
        found["safe"] = exponents_safe(facts_ref[0:1], key_norms, head_size)

    def keep(head, queries, sums):
        found[head, queries.start] = sums

    def store(head, queries, sums):
        sums = sums + found.pop((head, queries.start))
        y_ref[head * head_size : (head + 1) * head_size, queries] = divided(sums, head_size)

    def own_part(start):
        mine = start // half * half
        return [(k_ref, vt_ref, mine, mine + half)]

    def arrived_part(start):
        other = half - start // half * half
        return [(kr_ref, vr_ref, other, other + half)]

    def attend(parts_of, finish):
        return attention_jobs(
            qt_ref, range(0, rows, QUERY_BLOCK), range(HEADS), parts_of, head_size, finish
        )

    jobs = attend(own_part, keep)
    jobs.insert(PREPARE_AFTER, (lambda: None, prepare))
    run_jobs(jobs + attend(arrived_part, store))
    safe = found["safe"]
    run_jobs(output.jobs(0, rows), ahead=1)
    output.wait()

    @pl.when(jnp.logical_not(safe))
    def _():
        for start in (0, half):
            mine, other = slice(start, start + half), slice(half - start, rows - start)
            shifted_attention(
                qt_ref,
                start,
                half,
                [
                    lambda tile, head, mine=mine: (k_ref[mine, tile], vt_ref[head, :, mine]),
                    lambda tile, head, other=other: (kr_ref[other, tile], vr_ref[head, :, other]),
                ],
                head_size,
                y_ref,
            )
        run_jobs(output.jobs(0, rows), ahead=1)
        output.wait()


def finish_kernel(
    lanes, clusters, dest_ref, points_ref, near_ref, far_ref, wo_ref, gain_ref, up_ref, down_ref,
    out_ref, done_ref, slots, counts, origin, sems,
):
    places, _ = packed_places(dest_ref, clusters, lanes, slots, counts)
    output = OutputRows(
        places, points_ref, near_ref, far_ref, wo_ref, gain_ref, up_ref, down_ref, out_ref,
        done_ref, origin, sems,
    )
    run_jobs(output.jobs(0, output.rows), ahead=1)
    output.wait()


def owner_far_kernel(head_size, x_ref, gain_ref, wqk_ref, wv_ref, out_ref, qt, k, vt, y):
    rows, columns = x_ref.shape
    normed = rms_norm(x_ref[...], gain_ref[...])
    paired = dot32(normed, wqk_ref[...]).astype(bf16)
    values = dot32(normed, wv_ref[...]).astype(bf16)
    qt[...] = paired[:, :columns].T
    k[...] = paired[:, columns:]
    for head, extended in enumerate(extended_values(values, head_size)):
        vt[head] = extended
    shifted_attention(
        qt, 0, rows, [lambda tile, head: (k[:, tile], vt[head])], head_size, y
    )
    out_ref[...] = y[...].T


def per_device(
    points, gain_attn, w_query_key, w_value, w_out, gain_mlp, w_up, w_down, cluster_dest
):
    columns = points.shape[-1]
    flat = points.reshape(-1, columns)
    rows = flat.shape[0]
    lanes, regions = lax.axis_size("ball"), lax.axis_size("region")
    clusters = rows // CLUSTER
    share = 2 * clusters // lanes * CLUSTER
    owners = rows // share
    pooled = rows // POOL
    head_size = columns // HEADS
    tall = head_size + 16
    kept = head_size + 8
    dest = cluster_dest.reshape(clusters)
    gain_first = gain_attn.reshape(1, columns)
    gain_second = gain_mlp.reshape(1, columns)
    wide = jax.ShapeDtypeStruct((rows, columns), bf16)
    turned = jax.ShapeDtypeStruct((columns, rows), bf16)
    extended = jax.ShapeDtypeStruct((HEADS, tall, rows), bf16)
    scalars = [pltpu.SMEM((lanes,), jnp.int32)] * 2

    def attention_cost(queries, keys, heads):
        return cost(3 * heads * queries * keys * 256, 4 * rows * columns, heads * queries * keys)

    def shift(data, offset):
        return lax.ppermute(data, "ball", [(i, (i + offset) % lanes) for i in range(lanes)])

    row_of_gains = jax.ShapeDtypeStruct((1, columns), f32)
    packed, gain_first, gain_second, dest = pl.pallas_call(
        functools.partial(pack_kernel, lanes, clusters),
        out_shape=[wide, row_of_gains, row_of_gains, jax.ShapeDtypeStruct(dest.shape, jnp.int32)],
        in_specs=[in_hbm()] * 4,
        out_specs=[anywhere()] * 4,
        scratch_shapes=[pltpu.SMEM((clusters,), jnp.int32)]
        + scalars
        + [pltpu.SemaphoreType.DMA((clusters + 4,))],
        cost_estimate=cost(0, 4 * rows * columns),
        compiler_params=params(),
        name="pack",
    )(
        *(
            pltpu.with_memory_space_constraint(held, pltpu.HBM)
            for held in (dest, flat, gain_first, gain_second)
        )
    )

    pair_path = owners == 2 and lanes == 4
    if pair_path:
        from_across = shift(packed, 2)
        from_next = shift(packed[:share], lanes - 1)
        from_prior = shift(packed[share:], 1)

    query, keys, values, pool, facts = pl.pallas_call(
        functools.partial(project_kernel, head_size),
        out_shape=[
            turned,
            wide,
            extended,
            jax.ShapeDtypeStruct((2 * pooled, columns), bf16),
            jax.ShapeDtypeStruct((8, TILE), f32),
        ],
        in_specs=[in_vmem()] * 4,
        out_specs=[in_vmem()] * 5,
        cost_estimate=cost(6 * rows * columns * columns, 10 * rows * columns),
        compiler_params=params(),
        name="project",
    )(packed, gain_first, w_query_key, w_value)

    def across_regions(data, mask):
        return lax.ppermute(data, "region", [(i, i ^ mask) for i in range(regions)])

    gathered = pool.reshape(1, 2 * pooled, columns)
    step = regions // 2
    while step:
        gathered = jnp.concatenate([gathered, across_regions(gathered, step)], axis=0)
        step //= 2
    partial = [
        pl.pallas_call(
            functools.partial(near_part_kernel, heads, head_size),
            out_shape=jax.ShapeDtypeStruct((len(heads), kept, rows), f32),
            in_specs=[in_vmem()] * 3,
            out_specs=in_vmem(),
            cost_estimate=attention_cost(rows, rows, HEADS // 2),
            compiler_params=params(),
            name="near_part",
        )(query, keys, values)
        for heads in (range(FIRST_HEADS), range(FIRST_HEADS, HEADS))
    ]

    near = pl.pallas_call(
        functools.partial(near_kernel, head_size),
        out_shape=turned,
        in_specs=[in_vmem()] * (5 + len(partial)),
        out_specs=in_vmem(),
        scratch_shapes=[
            pltpu.VMEM((regions * pooled, columns), bf16),
            pltpu.VMEM((HEADS, tall, regions * pooled), bf16),
        ],
        cost_estimate=attention_cost(rows, regions * pooled, HEADS),
        compiler_params=params(),
        name="near",
    )(query, keys, values, facts, gathered, *partial)

    last_scratch = (
        [pltpu.VMEM((rows, columns), bf16)]
        + scalars
        + [pltpu.SMEM((clusters,), jnp.int32), pltpu.SemaphoreType.DMA((clusters,))]
    )
    if pair_path:
        block_out = pl.pallas_call(
            functools.partial(far_finish_kernel, lanes, clusters, head_size),
            out_shape=wide,
            in_specs=[in_smem()] + [in_vmem()] * 16,
            out_specs=anywhere(),
            scratch_shapes=[
                pltpu.VMEM((rows, columns), bf16),
                pltpu.VMEM((HEADS, tall, rows), bf16),
                pltpu.VMEM((columns, rows), bf16),
            ]
            + last_scratch,
            cost_estimate=attention_cost(rows, rows, HEADS),
            compiler_params=params(),
            name="far_finish",
        )(
            dest, packed, near, from_next, from_prior, from_across, query, keys, values, facts,
            gain_first, gain_second, w_query_key, w_value, w_out, w_up, w_down,
        )
    else:
        targets = dest // clusters
        members = lax.rem(targets - lax.axis_index("ball") + lanes, lanes)
        present = jnp.zeros((lanes,), jnp.int32).at[members].set(1)
        slot = jnp.cumsum(present) - present
        blocks = packed.reshape(owners, share, columns)
        empty = jnp.zeros((owners, share, columns), bf16)
        arrived, back = empty, empty

        def picked(source, offset):
            return lax.dynamic_index_in_dim(source, jnp.minimum(slot[offset], owners - 1), 0, False)

        def put(target, offset, block):
            index = jnp.minimum(slot[offset], owners - 1)
            placed = lax.dynamic_update_index_in_dim(target, block, index, 0)
            return jnp.where(present[offset] == 1, placed, target)

        for offset in range(lanes):
            block = picked(blocks, offset)
            arrived = put(arrived, offset, shift(block, offset) if offset else block)
        far_rotated = pl.pallas_call(
            functools.partial(owner_far_kernel, head_size),
            out_shape=wide,
            in_specs=[in_vmem()] * 4,
            out_specs=in_vmem(),
            scratch_shapes=[
                pltpu.VMEM((columns, rows), bf16),
                pltpu.VMEM((rows, columns), bf16),
                pltpu.VMEM((HEADS, tall, rows), bf16),
                pltpu.VMEM((columns, rows), bf16),
            ],
            cost_estimate=attention_cost(rows, rows, HEADS),
            compiler_params=params(),
            name="owner_far",
        )(arrived.reshape(rows, columns), gain_first, w_query_key, w_value)
        leaving = far_rotated.reshape(owners, share, columns)
        for offset in range(lanes):
            block = picked(leaving, offset)
            back = put(back, offset, shift(block, lanes - offset) if offset else block)
        block_out = pl.pallas_call(
            functools.partial(finish_kernel, lanes, clusters),
            out_shape=wide,
            in_specs=[in_smem()] + [in_vmem()] * 7,
            out_specs=anywhere(),
            scratch_shapes=last_scratch,
            cost_estimate=cost(20 * rows * columns * columns, 8 * rows * columns),
            compiler_params=params(),
            name="finish",
        )(
            dest, packed, near, back.reshape(rows, columns).T, w_out, gain_second, w_up, w_down
        )
    return block_out.reshape(points.shape)


def solution(mesh):
    placed = (
        P("ball", "region", None, None),
        P(),
        P(),
        P(),
        P(),
        P(),
        P(),
        P(),
        P("ball", "region", None),
    )
    return jax.shard_map(
        per_device,
        mesh=mesh,
        in_specs=placed,
        out_specs=P("ball", "region", None, None),
        check_vma=False,
    )
```
